256 devices in a mesh: dp: 2 (over core), expert: 4 (over x), tensor: 32 (over z, y).
Axes of the slice: x: 4, y: 4, z: 8, core: 2. Of those that a mesh axis runs over, the one named last changes fastest.
Arguments:
- tokens: bfloat16 [1024, 2304], P(('dp', 'expert'), 'tensor'), may hold values from -6 to 6
- expert_ids: int32 [1024, 2], P(('dp', 'expert')), may hold values from 0 to 3, all different within a row; in each aligned block of 128 rows (0 to 127, 128 to 255, ...) at most 96 rows name the same one
- router: bfloat16 [2304, 4], P('tensor'), may hold values from -0.125 to 0.125
- w_gate: bfloat16 [4, 2304, 6144], P('expert', None, 'tensor'), may hold values from -0.125 to 0.125
- w_up: bfloat16 [4, 2304, 6144], P('expert', None, 'tensor'), may hold values from -0.125 to 0.125
- w_down: bfloat16 [4, 6144, 2304], P('expert', 'tensor'), may hold values from -0.078125 to 0.078125
- cotangent: bfloat16 [1024, 2304], P(('dp', 'expert'), 'tensor'), may hold values from -6 to 6
Outputs:
- mixed: bfloat16 [1024, 2304], P(('dp', 'expert'), 'tensor')
- token_grad: bfloat16 [1024, 2304], P(('dp', 'expert'), 'tensor')
- router_grad: float32 [2304, 4], P('tensor')
- down_grad: float32 [4, 6144, 2304], P('expert', 'tensor')
The draws below stay inside these ranges and needn't reach their ends.
Inputs may be any that keep to these rules, and one draw needn't show every extreme that they name: `expert_ids`: the two ids of a token differ. In each aligned block of 128 rows (the tokens of one group), no expert is named by more than 96 assignments, a bound that some block reaches.
All inputs are finite; a program needn't handle non-finite values.
Results may differ from the reference program's by a relative error of at most 0.022.
Values may be sent and summed in bfloat16 or wider, within the bound.
No kernel may reach another device: no remote copies, remote signals or barrier semaphores. Data moves between devices by JAX's collectives and lax.ppermute only.
A program may use at most 64 MiB of HBM per device.

```python
import math
import jax
import jax.numpy as jnp
import numpy as np
from jax import lax

D = 2304
FF = 6144
TOK_GROUP = 128
EXPERTS = 4
CAP = 96
TOKENS = 1024
N_DP = 2
N_EXPERT = 4
N_TENSOR = 32


def steps_of(own_key, shape, cuts, least, largest):
    def one(dim, shards_of):
        heights = jax.random.uniform(jax.random.fold_in(jax.random.fold_in(own_key, 6), dim), (shards_of,), jnp.float32, least / len(cuts), largest / len(cuts))
        return jnp.repeat(jnp.exp(heights), shape[dim] // shards_of).reshape((-1,) + (1,) * (len(shape) - dim - 1))

    gain = one(*cuts[0])
    for cut in cuts[1:]:
        gain = gain * one(*cut)
    return gain


def deal_out(rng, own, number, rows, number_of, top, limit, skew):
    sequence = jax.random.permutation(rng, number_of)
    packed, common = portions_of(number_of, rows * top, limit, skew, True), portions_of(number_of, rows * top, limit, skew, False)
    places = jnp.arange(number_of)

    def named(sizes, rotation):
        used = int((sizes > 0).sum())
        fixed = max(1, used // 4)
        passed = fixed + (places - fixed + rotation * (used - fixed)) % max(1, number_of - fixed)
        return jnp.zeros((number_of,), jnp.int32).at[sequence[jnp.where(places < fixed, places, passed)]].set(jnp.asarray(sizes, jnp.int32))

    sizes = jnp.where(number % 4 == 0, named(packed, number // 4), named(common, number - number // 4 - 1))
    mixed = jax.random.permutation(jax.random.fold_in(own, 3), number_of)
    donor, sink = mixed[0:number_of // 2 * 2:2], mixed[1:number_of // 2 * 2:2]
    room = jnp.minimum(sizes[donor] - 1, limit - sizes[sink]) // 2
    room = jnp.where((donor == sequence[0]) | (sink == sequence[0]) | (sizes[sink] == 0), 0, jnp.maximum(room, 0))
    passed = jax.random.randint(jax.random.fold_in(own, 4), (number_of // 2,), 0, 1 << 20) % (room + 1)
    sizes = sizes.at[donor].add(-passed).at[sink].add(passed)
    items = jnp.searchsorted(jnp.cumsum(sizes), jnp.arange(rows * top), side="right").astype(jnp.int32)
    table = items.reshape(top, rows).T
    table = table[jax.random.permutation(jax.random.fold_in(own, 1), rows)]
    rotation = jax.random.randint(jax.random.fold_in(own, 2), (rows, 1), 0, top)
    return jnp.take_along_axis(table, (jnp.arange(top)[None, :] + rotation) % top, axis=1)


def portions_of(count, total, bound, slope, full):
    portions = [(1 << 20) // math.isqrt(grade ** slope) + 1 for grade in range(1, count + 1)]
    largest = bound if full else min(bound, max(-(-total // count), total * portions[0] // sum(portions)))
    least = 1 if total - largest >= count - 1 else 0
    counts, surplus = [largest] + [least] * (count - 1), total - largest - least * (count - 1)
    while surplus > 0:
        candidates = [i for i in range(1, count) if counts[i] < largest] or [i for i in range(1, count) if counts[i] < bound]
        pool, remaining = sum([portions[i] for i in candidates]), surplus
        for i in candidates:
            extra = min(bound - counts[i], max(1, remaining * portions[i] // pool), surplus)
            counts[i] = counts[i] + extra
            surplus = surplus - extra
    return np.array(counts)


def bell_draw(key, shape, deviation, reach, shards=(), kind=jnp.bfloat16):
    entries = jax.random.normal(key, shape, jnp.float32) * deviation
    if len(shards) > 0:
        entries = steps_of(key, shape, shards, -0.22, 0.18) * entries
    return jnp.clip(entries, min=-reach, max=reach).astype(kind)


def setup_inputs(seed: int = 0) -> dict:
    seeds = jax.random.split(jax.random.key(seed), 8)
    tokens = bell_draw(seeds[0], (TOKENS, D), 1.0, 6.0, ((0, 8), (1, 32)))
    expert_ids_keys = jax.random.split(jax.random.fold_in(seeds[1], 1), TOKENS // TOK_GROUP)
    expert_ids_turns = jax.random.permutation(jax.random.fold_in(seeds[1], 3), TOKENS // TOK_GROUP)
    expert_ids = jax.vmap(lambda own, number: deal_out(jax.random.fold_in(seeds[1], 2), own, number, TOK_GROUP, EXPERTS, 2, CAP, 2))(expert_ids_keys, expert_ids_turns).reshape((TOKENS, 2))
    router = bell_draw(seeds[2], (D, EXPERTS), D ** -0.5, 0.125, ((0, 32),))
    w_gate = bell_draw(seeds[3], (EXPERTS, D, FF), D ** -0.5, 0.125, ((0, 4), (2, 32)))
    w_up = bell_draw(seeds[4], (EXPERTS, D, FF), D ** -0.5, 0.125, ((0, 4), (2, 32)))
    w_down = bell_draw(seeds[5], (EXPERTS, FF, D), FF ** -0.5, 0.078125, ((0, 4), (1, 32)))
    cotangent = bell_draw(seeds[6], (TOKENS, D), 1.0, 6.0, ((0, 8), (1, 32)))
    return {"tokens": tokens, "expert_ids": expert_ids, "router": router, "w_gate": w_gate, "w_up": w_up, "w_down": w_down, "cotangent": cotangent}


def slot_table(block_ids, experts, capacity):
    flat = block_ids.reshape(-1)
    onehot = (flat[:, None] == jnp.arange(experts, dtype=jnp.int32)[None, :]).astype(jnp.int32)
    before = jnp.cumsum(onehot, axis=0) - onehot
    target = flat * capacity + jnp.sum(before * onehot, axis=1)
    place = (target[:, None] == jnp.arange(experts * capacity, dtype=jnp.int32)[None, :]).astype(jnp.float32)
    return place, onehot.astype(jnp.float32)


def split_sum(left, right, pieces):
    count, inner = left.shape
    width = right.shape[1]
    left_blocks = left.reshape(count, pieces, inner // pieces).astype(jnp.float32)
    right_blocks = right.reshape(pieces, inner // pieces, width).astype(jnp.float32)
    partial_value = jnp.einsum("mjk,jkf->jmf", left_blocks, right_blocks, precision=lax.Precision.HIGHEST)
    rounded = lax.optimization_barrier(partial_value.astype(jnp.bfloat16))
    return jnp.sum(rounded.astype(jnp.float32), axis=0)


def expert_pass(item):
    rows_x, rows_g, wg, wu, wd = item
    count = rows_x.shape[0]
    gate = jnp.dot(rows_x, wg, preferred_element_type=jnp.float32)
    up = jnp.dot(rows_x, wu, preferred_element_type=jnp.float32)
    sig = jax.nn.sigmoid(gate)
    hidden = (gate * sig * up).astype(jnp.bfloat16)
    out = split_sum(hidden, wd, N_TENSOR).astype(jnp.bfloat16)
    down_part = jnp.dot(hidden.T, rows_g, preferred_element_type=jnp.float32)
    dhid = jnp.dot(rows_g, wd.T, preferred_element_type=jnp.float32)
    grad_gate = (dhid * up * (sig * (1.0 + gate * (1.0 - sig)))).astype(jnp.bfloat16)
    grad_up = (dhid * (gate * sig)).astype(jnp.bfloat16)
    share = FF // N_TENSOR
    gate_blocks = grad_gate.reshape(count, N_TENSOR, share).astype(jnp.float32)
    up_blocks = grad_up.reshape(count, N_TENSOR, share).astype(jnp.float32)
    wg_blocks = wg.reshape(D, N_TENSOR, share).astype(jnp.float32)
    wu_blocks = wu.reshape(D, N_TENSOR, share).astype(jnp.float32)
    partial_value = jnp.einsum("mjf,djf->jmd", gate_blocks, wg_blocks, precision=lax.Precision.HIGHEST)
    partial_value = partial_value + jnp.einsum("mjf,djf->jmd", up_blocks, wu_blocks, precision=lax.Precision.HIGHEST)
    rounded = lax.optimization_barrier(partial_value.astype(jnp.bfloat16))
    rows_back = jnp.sum(rounded.astype(jnp.float32), axis=0).astype(jnp.bfloat16)
    return out, rows_back, down_part


def reference(tokens, expert_ids, router, w_gate, w_up, w_down, cotangent):
    groups = N_DP * N_EXPERT
    rows = TOK_GROUP
    x = tokens.reshape(groups, rows, D)
    dy = cotangent.reshape(groups, rows, D)
    ids = expert_ids.reshape(groups, rows, 2)
    place, onehot = jax.vmap(lambda b: slot_table(b, EXPERTS, CAP))(ids)
    pick = onehot.reshape(groups, rows, 2, EXPERTS)
    logits = jnp.einsum("grd,de->gre", x.astype(jnp.float32), router.astype(jnp.float32), precision=lax.Precision.HIGHEST)
    chosen = jnp.sum(logits[:, :, None, :] * pick, axis=-1)
    gap = chosen[:, :, 0] - chosen[:, :, 1]
    first = jax.nn.sigmoid(gap)
    second = jax.nn.sigmoid(-gap)
    gates = jnp.stack([first, second], axis=-1)
    xk = jnp.repeat(x, 2, axis=1).astype(jnp.float32)
    send_x = jnp.einsum("gsc,gsd->gcd", place, xk, precision=lax.Precision.HIGHEST).astype(jnp.bfloat16)
    out_grad = (gates[:, :, :, None] * dy.astype(jnp.float32)[:, :, None, :]).reshape(groups, 2 * rows, D).astype(jnp.bfloat16)
    send_g = jnp.einsum("gsc,gsd->gcd", place, out_grad.astype(jnp.float32), precision=lax.Precision.HIGHEST).astype(jnp.bfloat16)
    per_x = send_x.reshape(groups, EXPERTS, CAP, D).transpose(1, 0, 2, 3).reshape(EXPERTS, groups * CAP, D)
    per_g = send_g.reshape(groups, EXPERTS, CAP, D).transpose(1, 0, 2, 3).reshape(EXPERTS, groups * CAP, D)
    outs, backs, down_grad = lax.map(expert_pass, (per_x, per_g, w_gate, w_up, w_down))
    outs = outs.reshape(EXPERTS, groups, CAP, D).transpose(1, 0, 2, 3).reshape(groups, EXPERTS * CAP, D)
    backs = backs.reshape(EXPERTS, groups, CAP, D).transpose(1, 0, 2, 3).reshape(groups, EXPERTS * CAP, D)
    picked = jnp.einsum("gsc,gcd->gsd", place, outs.astype(jnp.float32), precision=lax.Precision.HIGHEST).reshape(groups, rows, 2, D)
    mixed = jnp.sum(gates[:, :, :, None] * picked, axis=2).astype(jnp.bfloat16)
    gate_grad = jnp.sum(dy.astype(jnp.float32)[:, :, None, :] * picked, axis=-1)
    gap_grad = (gate_grad[:, :, 0] - gate_grad[:, :, 1]) * first * second
    logit_grad = gap_grad[:, :, None] * (pick[:, :, 0, :] - pick[:, :, 1, :])
    rows_grad = jnp.einsum("gsc,gcd->gsd", place, backs.astype(jnp.float32), precision=lax.Precision.HIGHEST).reshape(groups, rows, 2, D)
    from_router = jnp.einsum("gre,de->grd", logit_grad, router.astype(jnp.float32), precision=lax.Precision.HIGHEST)
    token_grad = (rows_grad[:, :, 0, :] + rows_grad[:, :, 1, :] + from_router).astype(jnp.bfloat16)
    router_grad = jnp.einsum("grd,gre->de", x.astype(jnp.float32), logit_grad, precision=lax.Precision.HIGHEST)
    return mixed.reshape(TOKENS, D), token_grad.reshape(TOKENS, D), router_grad, down_grad
```

```python
import jax
import jax.numpy as jnp
from jax import lax
from jax.experimental import pallas as pl
from jax.experimental.pallas import tpu as pltpu
from jax.sharding import PartitionSpec as P

F32 = jnp.float32
BF16 = jnp.bfloat16
NZ, NY = 8, 4
NT = (((0,), (0,)), ((), ()))
LAST = (((1,), (1,)), ((), ()))


def dot(a, b, dims=(((1,), (0,)), ((), ()))):
    return lax.dot_general(a, b, dims, preferred_element_type=F32)


def iota(shape, axis):
    return lax.broadcasted_iota(jnp.int32, shape, axis)


def call(body, outs, *args, scalars=0, flops=0, name=None):
    smem = pl.BlockSpec(memory_space=pltpu.SMEM)
    vmem = pl.BlockSpec(memory_space=pltpu.VMEM)
    moved = sum(a.size * a.dtype.itemsize for a in args)
    return pl.pallas_call(
        body,
        out_shape=tuple(jax.ShapeDtypeStruct(s, d) for s, d in outs),
        in_specs=[smem] * scalars + [vmem] * (len(args) - scalars),
        out_specs=tuple(vmem for _ in outs),
        compiler_params=pltpu.CompilerParams(vmem_limit_bytes=50 * 1024 * 1024),
        cost_estimate=pl.CostEstimate(flops=flops, bytes_accessed=moved, transcendentals=0),
        name=name,
    )(*args)


def shift_x(x, k):
    return lax.ppermute(x, "expert", [(i, (i + k) % 4) for i in range(4)])


def shift_z(x, k):
    pairs = [(z * NY + y, (z + k) % NZ * NY + y) for z in range(NZ) for y in range(NY)]
    return lax.ppermute(x, "tensor", pairs)


def shift_y(x, k):
    pairs = [(z * NY + y, z * NY + (y + k) % NY) for z in range(NZ) for y in range(NY)]
    return lax.ppermute(x, "tensor", pairs)


def halves(rows):
    return (rows // 2 + 15) // 16 * 16


def gather(x, shift, n):
    got = {0: [x]}
    fwd = bwd = x
    half = n // 2
    for s in range(1, half):
        fwd, bwd = shift(fwd, 1), shift(bwd, -1)
        got[n - s], got[s] = [fwd], [bwd]
    cut = halves(x.shape[0])
    got[half] = [shift(fwd[:cut], 1), shift(bwd[cut:], -1)]
    return [piece for k in range(n) for piece in got[k]]


def add(a, b):
    return (a.astype(F32) + b.astype(F32)).astype(BF16)


def scatter(blocks, shift, n):
    half = n // 2
    cut = halves(blocks[0].shape[0])
    fwd, bwd = shift(blocks[half][:cut], 1), shift(blocks[half][cut:], -1)
    for s in range(half - 1, 0, -1):
        up, down = blocks[s], blocks[n - s]
        if s == half - 1:
            fwd = jnp.concatenate([add(up[:cut], fwd), up[cut:]], 0)
            bwd = jnp.concatenate([down[:cut], add(down[cut:], bwd)], 0)
        else:
            fwd, bwd = add(up, fwd), add(down, bwd)
        fwd, bwd = shift(fwd, 1), shift(bwd, -1)
    return blocks[0], fwd, bwd


def pack_body(tok, cot, ids, out):
    rows = iota((8, 128), 0)
    first = jnp.broadcast_to(ids[0:1, :].astype(F32), (8, 128))
    second = jnp.broadcast_to(ids[1:2, :].astype(F32), (8, 128))
    ext = jnp.where(rows == 0, first, jnp.where(rows == 1, second, 0.0))
    out[:, 0:128] = jnp.concatenate([tok[...].astype(F32), ext], 0).astype(BF16)
    out[:, 128:256] = jnp.concatenate([cot[...].astype(F32), jnp.zeros((8, 128), F32)], 0).astype(BF16)


def ranks(masks):
    earlier = (iota((128, 128), 0) < iota((128, 128), 1)).astype(F32).astype(BF16)
    return dot(masks.astype(BF16), earlier)


def route_body(me, r0, r1, r2, r3, router, tok_out, cot_out, sgn_out):
    expert = me[0].astype(F32)
    row8 = iota((8, 128), 0).astype(F32)
    raws = [r[...].astype(F32) for r in (r0, r1, r2, r3)]
    firsts = [r[72:73, 0:128] for r in raws]
    seconds = [r[73:74, 0:128] for r in raws]
    masks = [jnp.where((a == expert) | (b == expert), 1.0, 0.0) for a, b in zip(firsts, seconds)]
    stacked = jnp.zeros((8, 128), F32)
    for k in range(4):
        stacked = jnp.where(row8 == k, jnp.broadcast_to(masks[k], (8, 128)), stacked)
    rank = ranks(stacked)
    total = jnp.zeros((176, 384), F32)
    for k in range(4):
        raw, mask = raws[k], masks[k]
        other = firsts[k] + seconds[k] - expert
        logits = dot(router[...], raws[k][:, 0:128].astype(BF16))
        own = jnp.sum(jnp.where(row8 == expert, logits, 0.0), 0, keepdims=True)
        rest = jnp.sum(jnp.where(row8 == jnp.broadcast_to(other, (8, 128)), logits, 0.0), 0, keepdims=True)
        gap = jnp.broadcast_to(own - rest, (8, 128))
        hi = gap.astype(BF16).astype(F32)
        mid = (gap - hi).astype(BF16).astype(F32)
        low = gap - hi - mid
        ext = jnp.where(row8 == 0, hi, jnp.where(row8 == 1, mid, jnp.where(row8 == 2, low, 0.0)))
        sign = jnp.where(row8 == expert, 1.0, 0.0) - jnp.where(row8 == jnp.broadcast_to(other, (8, 128)), 1.0, 0.0)
        left = jnp.concatenate(
            [raw[0:72, 0:128], ext, raw[0:72, 128:256], jnp.zeros((8, 128), F32), sign, jnp.zeros((8, 128), F32)], 0
        ).astype(BF16)
        slot = jnp.where(mask > 0, rank[k : k + 1, :] + 96.0 * k, -1.0).astype(jnp.int32)
        place = jnp.where(iota((384, 128), 0) == jnp.broadcast_to(slot, (384, 128)), 1.0, 0.0).astype(BF16)
        total = total + dot(left, place, LAST)
    tok_out[...] = total[0:80].astype(BF16)
    cot_out[...] = total[80:160].astype(BF16)
    sgn_out[...] = total[160:168]


def weights_body(at, wg, wu, wd, g_out, u_out, d_out):
    for z in range(NZ):
        for y in range(NY):
            zr = lax.rem(z - at[0] + NZ, NZ)
            yr = lax.rem(y - at[1] + NY, NY)
            t = z * NY + y
            for w, out, index in (
                (wg, g_out, yr * NZ + zr),
                (wu, u_out, yr * NZ + zr),
                (wd, d_out, zr * NY + yr),
            ):
                block = w[72 * t : 72 * t + 72, :]
                out[index] = jnp.concatenate([block, jnp.zeros((8, 192), F32)], 0).astype(BF16)


def forward_body(pieces, *refs):
    toks, wg, wu, wd = refs[:pieces], refs[pieces], refs[pieces + 1], refs[pieces + 2]
    gate_out, up_out, hid_out, gap_out, part_out = refs[pieces + 3 :]
    gate = jnp.zeros((192, 384), F32)
    up = jnp.zeros((192, 384), F32)
    gap = jnp.zeros((8, 384), F32)
    at = 0
    for tok in toks:
        rows = tok.shape[0]
        x = tok[...]
        gate = gate + dot(wg[at : at + rows, :], x, NT)
        up = up + dot(wu[at : at + rows, :], x, NT)
        line = lax.rem(iota((8, rows), 1) + at, 80)
        pick = jnp.where((line >= 72) & (line < 75), 1.0, 0.0).astype(BF16)
        gap = gap + dot(pick, x)
        at += rows
    hidden = (gate * jax.nn.sigmoid(gate) * up).astype(BF16)
    gate_out[...] = gate
    up_out[...] = up
    hid_out[...] = hidden
    gap_out[...] = gap
    scale = jax.nn.sigmoid(gap[0:1, :])
    for i in range(8):
        part = dot(wd[320 * i : 320 * i + 320, :], hidden) * scale
        part_out[320 * i : 320 * i + 320, :] = part.astype(BF16)


def backward_body(pieces, *refs):
    cots = refs[:pieces]
    wg, wu, wd, gate_ref, up_ref, hid_ref, gap_ref = refs[pieces : pieces + 7]
    part_out, scaled_out = refs[pieces + 7 :]
    dhid = jnp.zeros((192, 384), F32)
    at = 0
    for cot in cots:
        rows = cot.shape[0]
        dhid = dhid + dot(wd[at : at + rows, :], cot[...], NT)
        at += rows
    gap = gap_ref[0:1, :]
    first, second = jax.nn.sigmoid(gap), jax.nn.sigmoid(-gap)
    gate, up = gate_ref[...], up_ref[...]
    hidden = hid_ref[...].astype(F32)
    slope = jnp.sum(hidden * dhid, 0, keepdims=True) * first * second
    dhid = dhid * first
    sig = jax.nn.sigmoid(gate)
    grad_gate = (dhid * up * (sig * (1.0 + gate * (1.0 - sig)))).astype(BF16)
    grad_up = (dhid * (gate * sig)).astype(BF16)
    scaled_out[...] = (hidden * first).astype(BF16)
    line = lax.rem(iota((640, 384), 0), 80)
    for i in range(4):
        part = dot(wg[640 * i : 640 * i + 640, :], grad_gate) + dot(wu[640 * i : 640 * i + 640, :], grad_up)
        part = jnp.where(line == 72, jnp.broadcast_to(slope, (640, 384)), part)
        part_out[640 * i : 640 * i + 640, :] = part.astype(BF16)


def down_body(pieces, at_ref, *refs):
    cots, scaled, out = refs[:pieces], refs[pieces], refs[pieces + 1]
    block = 0
    for cot in cots:
        part = dot(cot[...], scaled[...], LAST)
        for i in range(cot.shape[0] // 80):
            z = lax.rem(block // NY + at_ref[0], NZ)
            y = lax.rem(block % NY + at_ref[1], NY)
            out[z * NY + y] = part[80 * i : 80 * i + 80, :].astype(BF16)
            block += 1


def finish_body(o0, o1, o2, g0, g1, g2, sgn, router, tok, p0, p1, p2, p3):
    out = o0[...].astype(F32) + o1[...].astype(F32) + o2[...].astype(F32)
    grad = g0[...].astype(F32) + g1[...].astype(F32) + g2[...].astype(F32)
    delta = sgn[...] * grad[72:73, :]
    for j in range(4):
        grad = grad + router[:, j : j + 1] * delta[j : j + 1, :]
    hi = delta.astype(BF16)
    low = (delta - hi.astype(F32)).astype(BF16)
    share = dot(tok[...], hi, LAST) + dot(tok[...], low, LAST)
    share_hi = share.astype(BF16)
    share_low = (share - share_hi.astype(F32)).astype(BF16)
    row, lane = iota((8, 128), 0), iota((8, 128), 1)
    at_hi = jnp.where((lane == row + 96) & (row < 4), 1.0, 0.0).astype(BF16)
    at_low = jnp.where((lane == row + 100) & (row < 4), 1.0, 0.0).astype(BF16)
    extra = dot(share_hi, at_hi) + dot(share_low, at_low)
    extra = jnp.concatenate([extra, jnp.zeros((80, 128), F32)], 0)
    both = jnp.concatenate([out, grad], 0).astype(BF16)
    slot, lane = iota((384, 128), 0), iota((384, 128), 1)
    for k, ref in enumerate((p0, p1, p2, p3)):
        pick = jnp.where((slot == lane + 96 * k) & (lane < 96), 1.0, 0.0).astype(BF16)
        ref[...] = (dot(both, pick) + extra).astype(BF16)


def combine_body(me, ids, r0, r1, r2, r3, mixed_out, grad_out, share_out):
    row8 = iota((8, 128), 0)
    first = jnp.broadcast_to(ids[0:1, :], (8, 128))
    second = jnp.broadcast_to(ids[1:2, :], (8, 128))
    owner = lax.rem(me[0] - row8 + 8, 4)
    masks = jnp.where((first == owner) | (second == owner), 1.0, 0.0)
    rank = ranks(masks)
    slots = jnp.where(masks > 0, rank, -1.0).astype(jnp.int32)
    total = jnp.zeros((160, 128), F32)
    share = jnp.zeros((72, 128), F32)
    for k, ref in enumerate((r0, r1, r2, r3)):
        place = jnp.where(iota((128, 128), 0) == jnp.broadcast_to(slots[k : k + 1, :], (128, 128)), 1.0, 0.0)
        rows = ref[...]
        total = total + dot(rows, place.astype(BF16))
        share = share + rows[0:72, :].astype(F32)
    mixed_out[...] = total[0:72].astype(BF16)
    grad_out[...] = total[80:152].astype(BF16)
    share_out[...] = share


def on_device(tokens, expert_ids, router, w_gate, w_up, w_down, cotangent):
    me = lax.axis_index("expert").astype(jnp.int32).reshape(1)
    t = lax.axis_index("tensor").astype(jnp.int32)
    at = jnp.stack([t // NY, t % NY])
    ids = expert_ids.T
    router_wide = jnp.pad(router.T, ((0, 4), (0, 8)))
    router_tall = jnp.pad(router.astype(F32), ((0, 8), (0, 4)))

    (raw,) = call(pack_body, [((80, 256), BF16)], tokens.T, cotangent.T, ids, name="pack")
    raws = [raw] + [shift_x(raw, -k) for k in (1, 2, 3)]
    tok, cot, sgn = call(
        route_body,
        [((80, 384), BF16), ((80, 384), BF16), ((8, 384), F32)],
        me, *raws, router_wide, scalars=1, name="route",
    )

    wide = (32, 80, 192)
    wg, wu, wd = call(
        weights_body,
        [(wide, BF16)] * 3,
        at, w_gate[0].astype(F32), w_up[0].astype(F32), w_down[0].T.astype(F32), scalars=1, name="weights",
    )
    wg, wu, wd = wg.reshape(2560, 192), wu.reshape(2560, 192), wd.reshape(2560, 192)

    tok_z = jnp.concatenate(gather(tok, shift_z, NZ), 0)
    cot_y = jnp.concatenate(gather(cot, shift_y, NY), 0)
    toks = gather(tok_z, shift_y, NY)
    cots = gather(cot_y, shift_z, NZ)

    tall = (2560, 384)
    gate, up, hidden, gap, out_part = call(
        lambda *r: forward_body(len(toks), *r),
        [((192, 384), F32), ((192, 384), F32), ((192, 384), BF16), ((8, 384), F32), (tall, BF16)],
        *toks, wg, wu, wd, flops=1200000000, name="forward",
    )
    grad_part, scaled = call(
        lambda *r: backward_body(len(cots), *r),
        [(tall, BF16), ((192, 384), BF16)],
        *cots, wg, wu, wd, gate, up, hidden, gap, flops=1200000000, name="backward",
    )
    (down,) = call(
        lambda *r: down_body(len(cots), *r),
        [(wide, BF16)],
        at, *cots, scaled, scalars=1, flops=400000000, name="down",
    )

    out_z = [out_part[320 * i : 320 * i + 320] for i in range(NZ)]
    grad_y = [grad_part[640 * i : 640 * i + 640] for i in range(NY)]
    a, b, c = scatter(out_z, shift_z, NZ)
    out_y = (a.astype(F32) + b.astype(F32) + c.astype(F32)).astype(BF16)
    a, b, c = scatter(grad_y, shift_y, NY)
    grad_z = (a.astype(F32) + b.astype(F32) + c.astype(F32)).astype(BF16)
    outs = scatter([out_y[80 * i : 80 * i + 80] for i in range(NY)], shift_y, NY)
    grads = scatter([grad_z[80 * i : 80 * i + 80] for i in range(NZ)], shift_z, NZ)

    down = down[:, :72, :].reshape(2304, 192).T
    other = lax.ppermute(down, "dp", [(0, 1), (1, 0)])
    down_grad = (down.astype(F32) + other.astype(F32))[None]

    parts = call(
        finish_body, [((160, 128), BF16)] * 4, *outs, *grads, sgn, router_tall, tok, name="finish"
    )
    back = [parts[0]] + [shift_x(parts[k], k) for k in (1, 2, 3)]
    mixed, token_grad, share = call(
        combine_body,
        [((72, 128), BF16), ((72, 128), BF16), ((72, 128), F32)],
        me, ids, *back, scalars=1, name="combine",
    )
    share = share[:, 96:100] + share[:, 100:104]
    router_grad = share + lax.ppermute(share, "dp", [(0, 1), (1, 0)])
    return mixed.T, token_grad.T, router_grad, down_grad


def solution(mesh):
    in_specs = (
        P(("dp", "expert"), "tensor"),
        P(("dp", "expert"), None),
        P("tensor", None),
        P("expert", None, "tensor"),
        P("expert", None, "tensor"),
        P("expert", "tensor", None),
        P(("dp", "expert"), "tensor"),
    )
    out_specs = (
        P(("dp", "expert"), "tensor"),
        P(("dp", "expert"), "tensor"),
        P("tensor", None),
        P("expert", "tensor", None),
    )
    return jax.shard_map(
        on_device, mesh=mesh, in_specs=in_specs, out_specs=out_specs, check_vma=False
    )
```

```python
import jax
import jax.numpy as jnp
from jax import lax
from jax.experimental import pallas as pl
from jax.experimental.pallas import tpu as pltpu
from jax.sharding import PartitionSpec as P

F32 = jnp.float32
BF16 = jnp.bfloat16
NZ, NY = 8, 4
NT = (((0,), (0,)), ((), ()))
LAST = (((1,), (1,)), ((), ()))


def dot(a, b, dims=(((1,), (0,)), ((), ()))):
    return lax.dot_general(a, b, dims, preferred_element_type=F32)


def iota(shape, axis):
    return lax.broadcasted_iota(jnp.int32, shape, axis)


def call(body, outs, *args, scalars=0, flops=0, name=None):
    smem = pl.BlockSpec(memory_space=pltpu.SMEM)
    vmem = pl.BlockSpec(memory_space=pltpu.VMEM)
    moved = sum(a.size * a.dtype.itemsize for a in args)
    return pl.pallas_call(
        body,
        out_shape=tuple(jax.ShapeDtypeStruct(s, d) for s, d in outs),
        in_specs=[smem] * scalars + [vmem] * (len(args) - scalars),
        out_specs=tuple(vmem for _ in outs),
        compiler_params=pltpu.CompilerParams(vmem_limit_bytes=50 * 1024 * 1024),
        cost_estimate=pl.CostEstimate(flops=flops, bytes_accessed=moved, transcendentals=0),
        name=name,
    )(*args)


def shift_x(x, k):
    return lax.ppermute(x, "expert", [(i, (i + k) % 4) for i in range(4)])


def ring_pairs(n):
    even = [i ^ 1 for i in range(n)]
    odd = [(i + 1) % n if i % 2 else (i - 1) % n for i in range(n)]
    opposite = [(i + n // 2) % n for i in range(n)]
    return even, odd, opposite


def swaps(along):
    n = NZ if along == "z" else NY
    moves = []
    for partner in ring_pairs(n):
        if along == "z":
            pairs = [(z * NY + y, partner[z] * NY + y) for z in range(NZ) for y in range(NY)]
        else:
            pairs = [(z * NY + y, z * NY + partner[y]) for z in range(NZ) for y in range(NY)]
        moves.append(lambda x, pairs=pairs: lax.ppermute(x, "tensor", pairs))
    return moves, n


def halves(rows):
    return (rows // 2 + 15) // 16 * 16


def gather(x, along):
    (even, odd, _), n = swaps(along)
    half = n // 2
    got = {0: [x]}
    a = b = x
    for s in range(1, half):
        a, b = even(b), odd(a)
        got[s], got[n - s] = [a], [b]
    cut = halves(x.shape[0])
    got[half] = [even(b[:cut]), odd(a[cut:])]
    return [piece for k in range(n) for piece in got[k]]


def add(a, b):
    return (a.astype(F32) + b.astype(F32)).astype(BF16)


def scatter(blocks, along, direct):
    (even, odd, opposite), n = swaps(along)
    half = n // 2
    terms = [blocks[0]]
    a, b = blocks[half - 1], blocks[n - half + 1]
    if direct:
        terms.append(opposite(blocks[half]))
    else:
        rows = blocks[0].shape[0]
        cut = halves(rows)
        c, d = even(blocks[half][:cut]), odd(blocks[half][cut:])
        zero = jnp.zeros((), BF16)
        a = add(a, lax.pad(d, zero, ((cut, 0, 0), (0, 0, 0))))
        b = add(b, lax.pad(c, zero, ((0, rows - cut, 0), (0, 0, 0))))
    for s in range(half - 1, 0, -1):
        c, d = even(a), odd(b)
        if s > 1:
            a, b = add(blocks[s - 1], d), add(blocks[n - s + 1], c)
    return terms + [c, d]


def total(terms):
    return sum(t[...].astype(F32) for t in terms)


def pack_body(tok, cot, ids, out):
    rows = iota((8, 128), 0)
    first = jnp.broadcast_to(ids[0:1, :].astype(F32), (8, 128))
    second = jnp.broadcast_to(ids[1:2, :].astype(F32), (8, 128))
    ext = jnp.where(rows == 0, first, jnp.where(rows == 1, second, 0.0))
    out[:, 0:128] = jnp.concatenate([tok[...].astype(F32), ext], 0).astype(BF16)
    out[:, 128:256] = jnp.concatenate([cot[...].astype(F32), jnp.zeros((8, 128), F32)], 0).astype(BF16)


def ranks(masks):
    earlier = (iota((128, 128), 0) < iota((128, 128), 1)).astype(F32).astype(BF16)
    return dot(masks.astype(BF16), earlier)


def route_body(me, r0, r1, r2, r3, router, tok_out, cot_out, sgn_out):
    expert = me[0].astype(F32)
    row8 = iota((8, 128), 0).astype(F32)
    raws = [r[...].astype(F32) for r in (r0, r1, r2, r3)]
    firsts = [r[72:73, 0:128] for r in raws]
    seconds = [r[73:74, 0:128] for r in raws]
    masks = [jnp.where((a == expert) | (b == expert), 1.0, 0.0) for a, b in zip(firsts, seconds)]
    stacked = jnp.zeros((8, 128), F32)
    for k in range(4):
        stacked = jnp.where(row8 == k, jnp.broadcast_to(masks[k], (8, 128)), stacked)
    rank = ranks(stacked)
    total = jnp.zeros((176, 384), F32)
    for k in range(4):
        raw, mask = raws[k], masks[k]
        other = firsts[k] + seconds[k] - expert
        logits = dot(router[...], raws[k][:, 0:128].astype(BF16))
        own = jnp.sum(jnp.where(row8 == expert, logits, 0.0), 0, keepdims=True)
        rest = jnp.sum(jnp.where(row8 == jnp.broadcast_to(other, (8, 128)), logits, 0.0), 0, keepdims=True)
        gap = jnp.broadcast_to(own - rest, (8, 128))
        hi = gap.astype(BF16).astype(F32)
        mid = (gap - hi).astype(BF16).astype(F32)
        low = gap - hi - mid
        ext = jnp.where(row8 == 0, hi, jnp.where(row8 == 1, mid, jnp.where(row8 == 2, low, 0.0)))
        sign = jnp.where(row8 == expert, 1.0, 0.0) - jnp.where(row8 == jnp.broadcast_to(other, (8, 128)), 1.0, 0.0)
        left = jnp.concatenate(
            [raw[0:72, 0:128], ext, raw[0:72, 128:256], jnp.zeros((8, 128), F32), sign, jnp.zeros((8, 128), F32)], 0
        ).astype(BF16)
        slot = jnp.where(mask > 0, rank[k : k + 1, :] + 96.0 * k, -1.0).astype(jnp.int32)
        place = jnp.where(iota((384, 128), 0) == jnp.broadcast_to(slot, (384, 128)), 1.0, 0.0).astype(BF16)
        total = total + dot(left, place, LAST)
    tok_out[...] = total[0:80].astype(BF16)
    cot_out[...] = total[80:160].astype(BF16)
    sgn_out[...] = total[160:168]


def distance(index, at, n):
    side = 1 - 2 * lax.rem(at, 2)
    return lax.rem(side * (index - at) + 2 * n, n)


def position(steps, at, n):
    side = 1 - 2 * lax.rem(at, 2)
    return lax.rem(at + side * steps + 2 * n, n)


def weights_body(at, wg, wu, wd, g_out, u_out, d_out):
    eye = jnp.where(iota((192, 192), 0) == iota((192, 192), 1), 1.0, 0.0).astype(BF16)
    zero = jnp.zeros((8, 192), F32)
    zs = [distance(z, at[0], NZ) for z in range(NZ)]
    ys = [distance(y, at[1], NY) for y in range(NY)]
    for w, out, z_first in ((wg, g_out, False), (wu, u_out, False), (wd, d_out, True)):
        for h in range(2):
            tall = dot(w[:, 1152 * h : 1152 * h + 1152], eye, NT)
            for i in range(16):
                z, y = zs[4 * h + i // NY], ys[i % NY]
                index = z * NY + y if z_first else y * NZ + z
                out[index] = jnp.concatenate([tall[72 * i : 72 * i + 72], zero], 0).astype(BF16)


def forward_body(pieces, *refs):
    toks, wg, wu, wd = refs[:pieces], refs[pieces], refs[pieces + 1], refs[pieces + 2]
    gate_out, up_out, hid_out, gap_out = refs[pieces + 3 : pieces + 7]
    parts = refs[pieces + 7 :]
    gate = jnp.zeros((192, 384), F32)
    up = jnp.zeros((192, 384), F32)
    gap = jnp.zeros((8, 384), F32)
    at = 0
    for tok in toks:
        rows = tok.shape[0]
        x = tok[...]
        gate = gate + dot(wg[at : at + rows, :], x, NT)
        up = up + dot(wu[at : at + rows, :], x, NT)
        line = lax.rem(iota((8, rows), 1) + at, 80)
        pick = jnp.where((line >= 72) & (line < 75), 1.0, 0.0).astype(BF16)
        gap = gap + dot(pick, x)
        at += rows
    hidden = (gate * jax.nn.sigmoid(gate) * up).astype(BF16)
    gate_out[...] = gate
    up_out[...] = up
    hid_out[...] = hidden
    gap_out[...] = gap
    scale = jax.nn.sigmoid(gap[0:1, :])
    for i, part in enumerate(parts):
        part[...] = (dot(wd[320 * i : 320 * i + 320, :], hidden) * scale).astype(BF16)


def backward_body(pieces, *refs):
    cots = refs[:pieces]
    wg, wu, wd, gate_ref, up_ref, hid_ref, gap_ref = refs[pieces : pieces + 7]
    scaled_out, parts = refs[pieces + 7], refs[pieces + 8 :]
    dhid = jnp.zeros((192, 384), F32)
    at = 0
    for cot in cots:
        rows = cot.shape[0]
        dhid = dhid + dot(wd[at : at + rows, :], cot[...], NT)
        at += rows
    gap = gap_ref[0:1, :]
    first, second = jax.nn.sigmoid(gap), jax.nn.sigmoid(-gap)
    gate, up = gate_ref[...], up_ref[...]
    hidden = hid_ref[...].astype(F32)
    slope = jnp.sum(hidden * dhid, 0, keepdims=True) * first * second
    dhid = dhid * first
    sig = jax.nn.sigmoid(gate)
    grad_gate = (dhid * up * (sig * (1.0 + gate * (1.0 - sig)))).astype(BF16)
    grad_up = (dhid * (gate * sig)).astype(BF16)
    scaled_out[...] = (hidden * first).astype(BF16)
    line = lax.rem(iota((640, 384), 0), 80)
    for i, out in enumerate(parts):
        part = dot(wg[640 * i : 640 * i + 640, :], grad_gate) + dot(wu[640 * i : 640 * i + 640, :], grad_up)
        out[...] = jnp.where(line == 72, jnp.broadcast_to(slope, (640, 384)), part).astype(BF16)


def down_body(pieces, at_ref, *refs):
    cots, scaled, out = refs[:pieces], refs[pieces], refs[pieces + 1]
    block = 0
    for cot in cots:
        part = dot(cot[...], scaled[...], LAST)
        for i in range(cot.shape[0] // 80):
            z = position(block // NY, at_ref[0], NZ)
            y = position(block % NY, at_ref[1], NY)
            out[z * NY + y] = part[80 * i : 80 * i + 80, :].astype(BF16)
            block += 1


def finish_body(outs, grads, *refs):
    sgn, router, tok, p0, p1, p2, p3 = refs[outs + grads :]
    out, grad = total(refs[:outs]), total(refs[outs : outs + grads])
    delta = sgn[...] * grad[72:73, :]
    for j in range(4):
        grad = grad + router[:, j : j + 1] * delta[j : j + 1, :]
    hi = delta.astype(BF16)
    low = (delta - hi.astype(F32)).astype(BF16)
    share = dot(tok[...], hi, LAST) + dot(tok[...], low, LAST)
    share_hi = share.astype(BF16)
    share_low = (share - share_hi.astype(F32)).astype(BF16)
    row, lane = iota((8, 128), 0), iota((8, 128), 1)
    at_hi = jnp.where((lane == row + 96) & (row < 4), 1.0, 0.0).astype(BF16)
    at_low = jnp.where((lane == row + 100) & (row < 4), 1.0, 0.0).astype(BF16)
    extra = dot(share_hi, at_hi) + dot(share_low, at_low)
    extra = jnp.concatenate([extra, jnp.zeros((80, 128), F32)], 0)
    both = jnp.concatenate([out, grad], 0).astype(BF16)
    slot, lane = iota((384, 128), 0), iota((384, 128), 1)
    for k, ref in enumerate((p0, p1, p2, p3)):
        pick = jnp.where((slot == lane + 96 * k) & (lane < 96), 1.0, 0.0).astype(BF16)
        ref[...] = (dot(both, pick) + extra).astype(BF16)


def combine_body(me, ids, r0, r1, r2, r3, mixed_out, grad_out, share_out):
    row8 = iota((8, 128), 0)
    first = jnp.broadcast_to(ids[0:1, :], (8, 128))
    second = jnp.broadcast_to(ids[1:2, :], (8, 128))
    owner = lax.rem(me[0] - row8 + 8, 4)
    masks = jnp.where((first == owner) | (second == owner), 1.0, 0.0)
    rank = ranks(masks)
    slots = jnp.where(masks > 0, rank, -1.0).astype(jnp.int32)
    total = jnp.zeros((160, 128), F32)
    share = jnp.zeros((72, 128), F32)
    for k, ref in enumerate((r0, r1, r2, r3)):
        place = jnp.where(iota((128, 128), 0) == jnp.broadcast_to(slots[k : k + 1, :], (128, 128)), 1.0, 0.0)
        rows = ref[...]
        total = total + dot(rows, place.astype(BF16))
        share = share + rows[0:72, :].astype(F32)
    mixed_out[...] = total[0:72].astype(BF16)
    grad_out[...] = total[80:152].astype(BF16)
    share_out[...] = share


def on_device(tokens, expert_ids, router, w_gate, w_up, w_down, cotangent):
    me = lax.axis_index("expert").astype(jnp.int32).reshape(1)
    t = lax.axis_index("tensor").astype(jnp.int32)
    at = jnp.stack([t // NY, t % NY])
    ids = expert_ids.T
    router_wide = jnp.pad(router.T, ((0, 4), (0, 8)))
    router_tall = jnp.pad(router.astype(F32), ((0, 8), (0, 4)))

    (raw,) = call(pack_body, [((80, 256), BF16)], tokens.T, cotangent.T, ids, name="pack")
    raws = [raw] + [shift_x(raw, -k) for k in (1, 2, 3)]
    tok, cot, sgn = call(
        route_body,
        [((80, 384), BF16), ((80, 384), BF16), ((8, 384), F32)],
        me, *raws, router_wide, scalars=1, name="route",
    )

    wide = (32, 80, 192)
    wg, wu, wd = call(
        weights_body, [(wide, BF16)] * 3, at, w_gate[0].T, w_up[0].T, w_down[0], scalars=1, name="weights"
    )
    wg, wu, wd = wg.reshape(2560, 192), wu.reshape(2560, 192), wd.reshape(2560, 192)

    tok_z = jnp.concatenate(gather(tok, "z"), 0)
    cot_y = jnp.concatenate(gather(cot, "y"), 0)
    toks = gather(tok_z, "y")
    cots = gather(cot_y, "z")

    square = (192, 384)
    gate, up, hidden, gap, *out_z = call(
        lambda *r: forward_body(len(toks), *r),
        [(square, F32), (square, F32), (square, BF16), ((8, 384), F32)] + [((320, 384), BF16)] * NZ,
        *toks, wg, wu, wd, flops=1200000000, name="forward",
    )
    scaled, *grad_y = call(
        lambda *r: backward_body(len(cots), *r),
        [(square, BF16)] + [((640, 384), BF16)] * NY,
        *cots, wg, wu, wd, gate, up, hidden, gap, flops=1200000000, name="backward",
    )
    (down,) = call(
        lambda *r: down_body(len(cots), *r),
        [(wide, BF16)],
        at, *cots, scaled, scalars=1, flops=400000000, name="down",
    )

    out_y = total(scatter(out_z, "z", False)).astype(BF16)
    grad_z = total(scatter(grad_y, "y", False)).astype(BF16)
    outs = scatter([out_y[80 * i : 80 * i + 80] for i in range(NY)], "y", True)
    grads = scatter([grad_z[80 * i : 80 * i + 80] for i in range(NZ)], "z", True)

    down = down[:, :72, :].reshape(2304, 192).T
    other = lax.ppermute(down, "dp", [(0, 1), (1, 0)])
    down_grad = (down.astype(F32) + other.astype(F32))[None]

    parts = call(
        lambda *r: finish_body(len(outs), len(grads), *r),
        [((160, 128), BF16)] * 4, *outs, *grads, sgn, router_tall, tok, name="finish"
    )
    back = [parts[0]] + [shift_x(parts[k], k) for k in (1, 2, 3)]
    mixed, token_grad, share = call(
        combine_body,
        [((72, 128), BF16), ((72, 128), BF16), ((72, 128), F32)],
        me, ids, *back, scalars=1, name="combine",
    )
    share = share[:, 96:100] + share[:, 100:104]
    router_grad = share + lax.ppermute(share, "dp", [(0, 1), (1, 0)])
    return mixed.T, token_grad.T, router_grad, down_grad


def solution(mesh):
    in_specs = (
        P(("dp", "expert"), "tensor"),
        P(("dp", "expert"), None),
        P("tensor", None),
        P("expert", None, "tensor"),
        P("expert", None, "tensor"),
        P("expert", "tensor", None),
        P(("dp", "expert"), "tensor"),
    )
    out_specs = (
        P(("dp", "expert"), "tensor"),
        P(("dp", "expert"), "tensor"),
        P("tensor", None),
        P("expert", "tensor", None),
    )
    return jax.shard_map(
        on_device, mesh=mesh, in_specs=in_specs, out_specs=out_specs, check_vma=False
    )
```

```python
import jax
import jax.numpy as jnp
from jax import lax
from jax.experimental import pallas as pl
from jax.experimental.pallas import tpu as pltpu
from jax.sharding import PartitionSpec as P

F32 = jnp.float32
BF16 = jnp.bfloat16
NZ, NY = 8, 4
NT = (((0,), (0,)), ((), ()))
LAST = (((1,), (1,)), ((), ()))


def dot(a, b, dims=(((1,), (0,)), ((), ()))):
    return lax.dot_general(a, b, dims, preferred_element_type=F32)


def iota(shape, axis):
    return lax.broadcasted_iota(jnp.int32, shape, axis)


def call(body, outs, *args, scalars=0, flops=0, limit=8, far=0, after=(), home=False, extra=(), name=None):
    smem = pl.BlockSpec(memory_space=pltpu.SMEM)
    vmem = pl.BlockSpec(memory_space=pltpu.VMEM)
    count = len(args)
    near = count - scalars - far
    moved = sum(a.size * a.dtype.itemsize for a in args)
    scratch = [pltpu.VMEM(a.shape, a.dtype) for a in args[count - far :]]
    if far:
        scratch.append(pltpu.SemaphoreType.DMA((far,)))
    scratch += [pltpu.VMEM(shape, dtype) for shape, dtype in extra]
    return pl.pallas_call(
        lambda *refs: body(*refs[:count], *refs[count + len(after) :]),
        out_shape=tuple(jax.ShapeDtypeStruct(s, d) for s, d in outs),
        in_specs=[smem] * scalars + [vmem] * near + [pl.BlockSpec(memory_space=pltpu.HBM)] * far
        + [pl.BlockSpec(memory_space=pl.ANY)] * len(after),
        out_specs=tuple(pl.BlockSpec() if home else vmem for _ in outs),
        scratch_shapes=scratch,
        compiler_params=pltpu.CompilerParams(vmem_limit_bytes=limit * 1024 * 1024),
        cost_estimate=pl.CostEstimate(flops=flops, bytes_accessed=moved, transcendentals=0),
        name=name,
    )(*args, *after)


def fetch(refs, held, sems):
    copies = [pltpu.make_async_copy(r, h, sems.at[i]) for i, (r, h) in enumerate(zip(refs, held))]
    for copy in copies:
        copy.start()
    return copies


def shift_x(x, k):
    return lax.ppermute(x, "expert", [(i, (i + k) % 4) for i in range(4)])


def ring_pairs(n):
    even = [i ^ 1 for i in range(n)]
    odd = [(i + 1) % n if i % 2 else (i - 1) % n for i in range(n)]
    opposite = [(i + n // 2) % n for i in range(n)]
    return even, odd, opposite


def swaps(along):
    n = NZ if along == "z" else NY
    moves = []
    for partner in ring_pairs(n):
        if along == "z":
            pairs = [(z * NY + y, partner[z] * NY + y) for z in range(NZ) for y in range(NY)]
        else:
            pairs = [(z * NY + y, z * NY + partner[y]) for z in range(NZ) for y in range(NY)]
        moves.append(lambda x, pairs=pairs: lax.ppermute(x, "tensor", pairs))
    return moves, n


def halves(rows):
    return (rows // 2 + 15) // 16 * 16


def cut_body(a, b, low, high):
    cut = low.shape[0]
    low[...] = b[:cut, :]
    high[...] = a[cut:, :]


def cut(a, b, after=()):
    rows, width = a.shape
    first = halves(rows)
    shape = [((first, width), BF16), ((rows - first, width), BF16)]
    return call(cut_body, shape, a, b, after=after, name="cut")


def relay_body(a, b, a_out, b_out):
    a_out[...] = b[...]
    b_out[...] = a[...]


def relay(a, b, after):
    return call(relay_body, [(a.shape, BF16)] * 2, a, b, after=after, name="relay")


def join_body(parts, *refs):
    at = 0
    for ref in refs[:parts]:
        rows = ref.shape[0]
        refs[parts][at : at + rows, :] = ref[...]
        at += rows


def join(pieces, after=()):
    rows = sum(p.shape[0] for p in pieces)
    shape = [((rows, pieces[0].shape[1]), BF16)]
    return call(lambda *r: join_body(len(pieces), *r), shape, *pieces, after=after, name="join")[0]


def add_body(a, b, c, d, a_out, b_out):
    cut = c.shape[0]
    rest = a.shape[0] - d.shape[0]
    if rest:
        a_out[:rest, :] = a[:rest, :]
        b_out[cut:, :] = b[cut:, :]
    a_out[rest:, :] = (a[rest:, :].astype(F32) + d[...].astype(F32)).astype(BF16)
    b_out[:cut, :] = (b[:cut, :].astype(F32) + c[...].astype(F32)).astype(BF16)


def add(a, b, c, d, after=()):
    return call(add_body, [(a.shape, BF16)] * 2, a, b, c, d, after=after, name="add")


def total(terms):
    return sum(t[...].astype(F32) for t in terms)


def split_body(terms, *refs):
    for i, out in enumerate(refs[terms:]):
        out[...] = total([r.at[80 * i : 80 * i + 80, :] for r in refs[:terms]]).astype(BF16)


def sum_blocks(*terms, after=()):
    shape = [((80, 384), BF16)] * (terms[0].shape[0] // 80)
    return call(lambda *r: split_body(len(terms), *r), shape, *terms, after=after, name="sum")


def ranks(masks):
    earlier = (iota((128, 128), 0) < iota((128, 128), 1)).astype(F32).astype(BF16)
    return dot(masks.astype(BF16), earlier)


def route_body(me, r0, r1, r2, r3, router, tok_out, cot_out, sgn_out):
    expert = me[0].astype(F32)
    row8 = iota((8, 128), 0).astype(F32)
    raws = [r[...].astype(F32) for r in (r0, r1, r2, r3)]
    firsts = [r[72:73, 0:128] for r in raws]
    seconds = [r[73:74, 0:128] for r in raws]
    masks = [jnp.where((a == expert) | (b == expert), 1.0, 0.0) for a, b in zip(firsts, seconds)]
    stacked = jnp.zeros((8, 128), F32)
    for k in range(4):
        stacked = jnp.where(row8 == k, jnp.broadcast_to(masks[k], (8, 128)), stacked)
    rank = ranks(stacked)
    total = jnp.zeros((176, 384), F32)
    for k in range(4):
        raw, mask = raws[k], masks[k]
        other = firsts[k] + seconds[k] - expert
        logits = dot(router[...], raws[k][:, 0:128].astype(BF16))
        own = jnp.sum(jnp.where(row8 == expert, logits, 0.0), 0, keepdims=True)
        rest = jnp.sum(jnp.where(row8 == jnp.broadcast_to(other, (8, 128)), logits, 0.0), 0, keepdims=True)
        gap = jnp.broadcast_to(own - rest, (8, 128))
        hi = gap.astype(BF16).astype(F32)
        mid = (gap - hi).astype(BF16).astype(F32)
        low = gap - hi - mid
        ext = jnp.where(row8 == 0, hi, jnp.where(row8 == 1, mid, jnp.where(row8 == 2, low, 0.0)))
        sign = jnp.where(row8 == expert, 1.0, 0.0) - jnp.where(row8 == jnp.broadcast_to(other, (8, 128)), 1.0, 0.0)
        left = jnp.concatenate(
            [raw[0:72, 0:128], ext, raw[0:72, 128:256], jnp.zeros((8, 128), F32), sign, jnp.zeros((8, 128), F32)], 0
        ).astype(BF16)
        slot = jnp.where(mask > 0, rank[k : k + 1, :] + 96.0 * k, -1.0).astype(jnp.int32)
        place = jnp.where(iota((384, 128), 0) == jnp.broadcast_to(slot, (384, 128)), 1.0, 0.0).astype(BF16)
        total = total + dot(left, place, LAST)
    tok_out[...] = total[0:80].astype(BF16)
    cot_out[...] = total[80:160].astype(BF16)
    sgn_out[...] = total[160:168]


def distance(index, at, n):
    side = 1 - 2 * lax.rem(at, 2)
    return lax.rem(side * (index - at) + 2 * n, n)


def position(steps, at, n):
    side = 1 - 2 * lax.rem(at, 2)
    return lax.rem(at + side * steps + 2 * n, n)


def weights_body(at, wg_ref, wu_ref, wd_ref, g_out, u_out, d_out, wg, wu, wd, sems):
    copies = fetch((wg_ref, wu_ref, wd_ref), (wg, wu, wd), sems)
    eye = jnp.where(iota((192, 192), 0) == iota((192, 192), 1), 1.0, 0.0).astype(BF16)
    zero = jnp.zeros((8, 192), F32)
    zs = [distance(z, at[0], NZ) for z in range(NZ)]
    ys = [distance(y, at[1], NY) for y in range(NY)]
    for copy, w, out, z_first in zip(copies, (wg, wu, wd), (g_out, u_out, d_out), (False, False, True)):
        copy.wait()
        for h in range(2):
            tall = dot(w[:, 1152 * h : 1152 * h + 1152], eye, NT)
            for i in range(16):
                z, y = zs[4 * h + i // NY], ys[i % NY]
                index = z * NY + y if z_first else y * NZ + z
                out[index] = jnp.concatenate([tall[72 * i : 72 * i + 72], zero], 0).astype(BF16)


def forward_body(pieces, *refs):
    toks, wg, wu, wd = refs[:pieces], refs[pieces], refs[pieces + 1], refs[pieces + 2]
    gate_out, up_out, hid_out, gap_out = refs[pieces + 3 : pieces + 7]
    parts = refs[pieces + 7 :]
    gate = jnp.zeros((192, 384), F32)
    up = jnp.zeros((192, 384), F32)
    gap = jnp.zeros((8, 384), F32)
    at = 0
    for tok in toks:
        rows = tok.shape[0]
        x = tok[...]
        gate = gate + dot(wg[at : at + rows, :], x, NT)
        up = up + dot(wu[at : at + rows, :], x, NT)
        line = lax.rem(iota((8, rows), 1) + at, 80)
        pick = jnp.where((line >= 72) & (line < 75), 1.0, 0.0).astype(BF16)
        gap = gap + dot(pick, x)
        at += rows
    hidden = (gate * jax.nn.sigmoid(gate) * up).astype(BF16)
    gate_out[...] = gate
    up_out[...] = up
    hid_out[...] = hidden
    gap_out[...] = gap
    scale = jax.nn.sigmoid(gap[0:1, :])
    at = 0
    for part in parts:
        rows = part.shape[0]
        part[...] = (dot(wd[at : at + rows, :], hidden) * scale).astype(BF16)
        at += rows


def backward_body(pieces, *refs):
    cots = refs[:pieces]
    wg, wu, wd, gate_ref, up_ref, hid_ref, gap_ref = refs[pieces : pieces + 7]
    scaled_out, parts = refs[pieces + 7], refs[pieces + 8 :]
    dhid = jnp.zeros((192, 384), F32)
    at = 0
    for cot in cots:
        rows = cot.shape[0]
        dhid = dhid + dot(wd[at : at + rows, :], cot[...], NT)
        at += rows
    gap = gap_ref[0:1, :]
    first, second = jax.nn.sigmoid(gap), jax.nn.sigmoid(-gap)
    gate, up = gate_ref[...], up_ref[...]
    hidden = hid_ref[...].astype(F32)
    slope = jnp.sum(hidden * dhid, 0, keepdims=True) * first * second
    dhid = dhid * first
    sig = jax.nn.sigmoid(gate)
    grad_gate = (dhid * up * (sig * (1.0 + gate * (1.0 - sig)))).astype(BF16)
    grad_up = (dhid * (gate * sig)).astype(BF16)
    scaled_out[...] = (hidden * first).astype(BF16)
    at = 0
    for out in parts:
        rows = out.shape[0]
        part = dot(wg[at : at + rows, :], grad_gate) + dot(wu[at : at + rows, :], grad_up)
        line = lax.rem(iota((rows, 384), 0), 80)
        out[...] = jnp.where(line == 72, jnp.broadcast_to(slope, (rows, 384)), part).astype(BF16)
        at += rows


def down_body(pieces, at_ref, *refs):
    cots, scaled, out, held = refs[:pieces], refs[pieces], refs[pieces + 1], refs[pieces + 2]
    block = 0
    for cot in cots:
        part = dot(cot[...], scaled[...], LAST)
        for i in range(cot.shape[0] // 80):
            z = position(block // NY, at_ref[0], NZ)
            y = position(block % NY, at_ref[1], NY)
            held[z * NY + y] = part[80 * i : 80 * i + 72, :]
            block += 1
    eye = jnp.where(iota((192, 192), 0) == iota((192, 192), 1), 1.0, 0.0).astype(BF16)
    tall = held[...].reshape(2304, 192).astype(BF16)
    out[...] = dot(eye, tall, LAST).astype(BF16)


def copy_body(x, out):
    out[...] = x[...]


def grad_body(mine, other, out, done):
    out[...] = mine[...].astype(F32) + other[...].astype(F32)
    done[...] = jnp.zeros((8, 128), F32)


def finish_body(outs, grads, *refs):
    sgn, router, tok, p0, p1, p2, p3 = refs[outs + grads :]
    out, grad = total(refs[:outs]), total(refs[outs : outs + grads])
    delta = sgn[...] * grad[72:73, :]
    hi = delta.astype(BF16)
    low = (delta - hi.astype(F32)).astype(BF16)
    grad = grad + dot(router[...], hi, NT) + dot(router[...], low, NT)
    rows = jnp.concatenate([tok[...], jnp.zeros((48, 384), BF16)], 0)
    share = dot(hi, rows, LAST) + dot(low, rows, LAST)
    share_hi = share.astype(BF16).astype(F32)
    share_low = pltpu.roll(share - share_hi, 4, 0)
    extra = jnp.where(iota((8, 128), 0) < 4, share_hi, share_low)
    extra = jnp.concatenate([jnp.zeros((72, 128), F32), extra, jnp.zeros((80, 128), F32)], 0)
    both = jnp.concatenate([out, grad], 0).astype(BF16)
    slot, lane = iota((384, 128), 0), iota((384, 128), 1)
    for k, ref in enumerate((p0, p1, p2, p3)):
        pick = jnp.where((slot == lane + 96 * k) & (lane < 96), 1.0, 0.0).astype(BF16)
        ref[...] = (dot(both, pick) + extra).astype(BF16)


def share_body(r0, r1, r2, r3, out):
    share = total([r.at[64:80, :] for r in (r0, r1, r2, r3)])[8:16]
    out[...] = share + pltpu.roll(share, 4, 0)


def combine_body(me, ids, r0, r1, r2, r3, mixed_out, grad_out):
    row8 = iota((8, 128), 0)
    first = jnp.broadcast_to(ids[0:1, :], (8, 128))
    second = jnp.broadcast_to(ids[1:2, :], (8, 128))
    owner = lax.rem(me[0] - row8 + 8, 4)
    masks = jnp.where((first == owner) | (second == owner), 1.0, 0.0)
    rank = ranks(masks)
    slots = jnp.where(masks > 0, rank, -1.0).astype(jnp.int32)
    both = jnp.zeros((160, 128), F32)
    for k, ref in enumerate((r0, r1, r2, r3)):
        place = jnp.where(iota((128, 128), 0) == jnp.broadcast_to(slots[k : k + 1, :], (128, 128)), 1.0, 0.0)
        both = both + dot(ref[...], place.astype(BF16))
    mixed_out[...] = both[0:72].astype(BF16)
    grad_out[...] = both[80:152].astype(BF16)


def on_device(tokens, expert_ids, router, w_gate, w_up, w_down, cotangent):
    me = lax.axis_index("expert").astype(jnp.int32).reshape(1)
    t = lax.axis_index("tensor").astype(jnp.int32)
    at = jnp.stack([t // NY, t % NY])
    ids = expert_ids.T
    router_wide = jnp.pad(router.T, ((0, 4), (0, 8)))

    rows = jnp.concatenate([tokens.T, cotangent.T], 1)
    raw = jnp.concatenate([rows, jnp.pad(ids.astype(BF16), ((0, 6), (0, 128)))], 0)
    (even_z, odd_z, far_z), (even_y, odd_y, far_y) = swaps("z")[0], swaps("y")[0]
    wide = (32, 80, 192)

    raws = [raw] + [shift_x(raw, -k) for k in (1, 2, 3)]
    wg, wu, wd = call(
        weights_body, [(wide, BF16)] * 3, at, w_gate[0].T, w_up[0].T, w_down[0],
        scalars=1, far=3, limit=16, name="weights",
    )
    tok, cot, sgn = call(
        route_body,
        [((80, 384), BF16), ((80, 384), BF16), ((8, 384), F32)],
        me, *raws, router_wide, scalars=1, after=[wg], name="route",
    )
    wg, wu, wd = wg.reshape(2560, 192), wu.reshape(2560, 192), wd.reshape(2560, 192)

    tz1, tz7, tz4 = even_z(tok), odd_z(tok), far_z(tok)
    cy1, cy3, cy2 = even_y(cot), odd_y(cot), far_y(cot)
    cot_y = join([cot, cy1, cy2, cy3])
    tz2, tz6 = even_z(tz7), odd_z(tz1)
    a, b = relay(tz2, tz6, after=[cy1, cy2, cy3, tz4])
    tz3, tz5 = even_z(a), odd_z(b)
    tok_z = join([tok, tz1, tz2, tz3, tz4, tz5, tz6, tz7])
    ty1, ty3 = even_y(tok_z), odd_y(tok_z)
    a, b = cut(ty1, ty3)
    ty2_low, ty2_high = even_y(a), odd_y(b)
    cz1, cz7 = even_z(cot_y), odd_z(cot_y)
    cz2, cz6 = even_z(cz7), odd_z(cz1)
    cz3, cz5 = even_z(cz6), odd_z(cz2)
    toks = [tok_z, ty1, ty2_low, ty2_high, ty3]

    square = (192, 384)
    gate, up, hidden, gap, *oz = call(
        lambda *r: forward_body(len(toks), *r),
        [(square, F32), (square, F32), (square, BF16), ((8, 384), F32)]
        + [((320 if i < 4 or i > 5 else 160, 384), BF16) for i in range(NZ + 1)],
        *toks, wg, wu, wd, flops=1200000000, limit=24, name="forward",
    )
    a, b = cut(cz3, cz5, after=[hidden])
    cz4_low, cz4_high = even_z(a), odd_z(b)
    cots = [cot_y, cz1, cz2, cz3, cz4_low, cz4_high, cz5, cz6, cz7]

    oz[4:6] = [oz[4:6]]
    c, d = even_z(oz[4][0]), odd_z(oz[4][1])
    scaled, *gy = call(
        lambda *r: backward_body(len(cots), *r),
        [(square, BF16)] + [((320 if i in (2, 3) else 640, 384), BF16) for i in range(NY + 1)],
        *cots, wg, wu, wd, gate, up, hidden, gap, flops=1200000000, limit=24, name="backward",
    )
    gy[2:4] = [gy[2:4]]
    a, b = add(oz[3], oz[5], c, d)
    e, f = even_y(gy[2][0]), odd_y(gy[2][1])
    g, h = add(gy[1], gy[3], e, f, after=[a])
    c, d = even_z(a), odd_z(b)
    (down,) = call(
        lambda *r: down_body(len(cots), *r),
        [((192, 2304), BF16)],
        at, *cots, scaled, scalars=1, flops=500000000, after=[g], extra=[((32, 72, 192), F32)],
        limit=16, name="down",
    )
    (mine,) = call(copy_body, [((192, 2304), BF16)], down, after=[c, d], name="copy")
    other = lax.ppermute(mine, "dp", [(0, 1), (1, 0)])
    a, b = add(oz[2], oz[6], c, d)
    e, f = even_y(g), odd_y(h)
    c, d = even_z(a), odd_z(b)
    gz = sum_blocks(gy[0], e, f)
    a, b = add(oz[1], oz[7], c, d)
    c, d = even_z(a), odd_z(b)
    e, f, gz_far = even_z(gz[3]), odd_z(gz[5]), far_z(gz[4])
    g, h = add(gz[2], gz[6], e, f)
    oy = sum_blocks(oz[0], c, d)
    outs = [oy[0], even_y(oy[1]), odd_y(oy[3]), far_y(oy[2])]
    e, f = even_z(g), odd_z(h)
    g, h = add(gz[1], gz[7], e, f)
    grads = [gz[0], gz_far, even_z(g), odd_z(h)]
    down_grad, done = call(
        grad_body, [((192, 2304), F32), ((8, 128), F32)], mine, other, home=True, limit=16, name="grad"
    )
    parts = call(
        lambda *r: finish_body(len(outs), len(grads), *r),
        [((160, 128), BF16)] * 4, *outs, *grads, sgn, router_wide, tok, name="finish",
    )
    back = [parts[0]] + [shift_x(parts[k], k) for k in (1, 2, 3)]
    (share,) = call(share_body, [((8, 128), F32)], *back, after=[done], name="share")
    mixed, token_grad = call(
        combine_body,
        [((72, 128), BF16), ((72, 128), BF16)],
        me, ids, *back, scalars=1, name="combine",
    )
    share = share + lax.ppermute(share, "dp", [(0, 1), (1, 0)])
    router_grad = share[:4, :72].T
    return mixed.T, token_grad.T, router_grad, down_grad[None]


def solution(mesh):
    in_specs = (
        P(("dp", "expert"), "tensor"),
        P(("dp", "expert"), None),
        P("tensor", None),
        P("expert", None, "tensor"),
        P("expert", None, "tensor"),
        P("expert", "tensor", None),
        P(("dp", "expert"), "tensor"),
    )
    out_specs = (
        P(("dp", "expert"), "tensor"),
        P(("dp", "expert"), "tensor"),
        P("tensor", None),
        P("expert", "tensor", None),
    )
    return jax.shard_map(
        on_device, mesh=mesh, in_specs=in_specs, out_specs=out_specs, check_vma=False
    )
```

```python
import jax
import jax.numpy as jnp
from jax import lax
from jax.experimental import pallas as pl
from jax.experimental.pallas import tpu as pltpu
from jax.sharding import PartitionSpec as P

F32 = jnp.float32
BF16 = jnp.bfloat16
NZ, NY = 8, 4
NT = (((0,), (0,)), ((), ()))
LAST = (((1,), (1,)), ((), ()))


def dot(a, b, dims=(((1,), (0,)), ((), ()))):
    return lax.dot_general(a, b, dims, preferred_element_type=F32)


def iota(shape, axis):
    return lax.broadcasted_iota(jnp.int32, shape, axis)


def call(body, outs, *args, scalars=0, flops=0, limit=8, far=0, after=(), home=False, extra=(), name=None):
    smem = pl.BlockSpec(memory_space=pltpu.SMEM)
    vmem = pl.BlockSpec(memory_space=pltpu.VMEM)
    count = len(args)
    near = count - scalars - far
    moved = sum(a.size * a.dtype.itemsize for a in args)
    scratch = [pltpu.VMEM(a.shape, a.dtype) for a in args[count - far :]]
    if far:
        scratch.append(pltpu.SemaphoreType.DMA((far,)))
    scratch += [pltpu.VMEM(shape, dtype) for shape, dtype in extra]
    return pl.pallas_call(
        lambda *refs: body(*refs[:count], *refs[count + len(after) :]),
        out_shape=tuple(jax.ShapeDtypeStruct(s, d) for s, d in outs),
        in_specs=[smem] * scalars + [vmem] * near + [pl.BlockSpec(memory_space=pltpu.HBM)] * far
        + [pl.BlockSpec(memory_space=pl.ANY)] * len(after),
        out_specs=tuple(pl.BlockSpec() if home else vmem for _ in outs),
        scratch_shapes=scratch,
        compiler_params=pltpu.CompilerParams(vmem_limit_bytes=limit * 1024 * 1024),
        cost_estimate=pl.CostEstimate(flops=flops, bytes_accessed=moved, transcendentals=0),
        name=name,
    )(*args, *after)


def fetch(refs, held, sems):
    copies = [pltpu.make_async_copy(r, h, sems.at[i]) for i, (r, h) in enumerate(zip(refs, held))]
    for copy in copies:
        copy.start()
    return copies


def shift_x(x, k):
    return lax.ppermute(x, "expert", [(i, (i + k) % 4) for i in range(4)])


def ring_pairs(n):
    even = [i ^ 1 for i in range(n)]
    odd = [(i + 1) % n if i % 2 else (i - 1) % n for i in range(n)]
    opposite = [(i + n // 2) % n for i in range(n)]
    return even, odd, opposite


def swaps(along):
    n = NZ if along == "z" else NY
    moves = []
    for partner in ring_pairs(n):
        if along == "z":
            pairs = [(z * NY + y, partner[z] * NY + y) for z in range(NZ) for y in range(NY)]
        else:
            pairs = [(z * NY + y, z * NY + partner[y]) for z in range(NZ) for y in range(NY)]
        moves.append(lambda x, pairs=pairs: lax.ppermute(x, "tensor", pairs))
    return moves, n


def halves(rows):
    return (rows // 2 + 15) // 16 * 16


def cut_body(a, b, low, high):
    cut = low.shape[0]
    low[...] = b[:cut, :]
    high[...] = a[cut:, :]


def cut(a, b, after=()):
    rows, width = a.shape
    first = halves(rows)
    shape = [((first, width), BF16), ((rows - first, width), BF16)]
    return call(cut_body, shape, a, b, after=after, name="cut")


def relay_body(a, b, a_out, b_out):
    a_out[...] = b[...]
    b_out[...] = a[...]


def relay(a, b, after):
    return call(relay_body, [(a.shape, BF16)] * 2, a, b, after=after, name="relay")


def join_body(parts, *refs):
    at = 0
    for ref in refs[:parts]:
        rows = ref.shape[0]
        refs[parts][at : at + rows, :] = ref[...]
        at += rows


def join(pieces, after=()):
    rows = sum(p.shape[0] for p in pieces)
    shape = [((rows, pieces[0].shape[1]), BF16)]
    return call(lambda *r: join_body(len(pieces), *r), shape, *pieces, after=after, name="join")[0]


def add_body(a, b, c, d, a_out, b_out):
    cut = c.shape[0]
    rest = a.shape[0] - d.shape[0]
    if rest:
        a_out[:rest, :] = a[:rest, :]
        b_out[cut:, :] = b[cut:, :]
    a_out[rest:, :] = (a[rest:, :].astype(F32) + d[...].astype(F32)).astype(BF16)
    b_out[:cut, :] = (b[:cut, :].astype(F32) + c[...].astype(F32)).astype(BF16)


def add(a, b, c, d, after=()):
    return call(add_body, [(a.shape, BF16)] * 2, a, b, c, d, after=after, name="add")


def total(terms):
    return sum(t[...].astype(F32) for t in terms)


def split_body(terms, *refs):
    for i, out in enumerate(refs[terms:]):
        out[...] = total([r.at[80 * i : 80 * i + 80, :] for r in refs[:terms]]).astype(BF16)


def sum_blocks(*terms, after=()):
    shape = [((80, 384), BF16)] * (terms[0].shape[0] // 80)
    return call(lambda *r: split_body(len(terms), *r), shape, *terms, after=after, name="sum")


def ranks(masks):
    earlier = (iota((128, 128), 0) < iota((128, 128), 1)).astype(F32).astype(BF16)
    return dot(masks.astype(BF16), earlier)


def route_body(me, r0, r1, r2, r3, router, tok_out, cot_out, sgn_out):
    expert = me[0].astype(F32)
    row8 = iota((8, 128), 0).astype(F32)
    raws = [r[...].astype(F32) for r in (r0, r1, r2, r3)]
    firsts = [r[72:73, 0:128] for r in raws]
    seconds = [r[73:74, 0:128] for r in raws]
    masks = [jnp.where((a == expert) | (b == expert), 1.0, 0.0) for a, b in zip(firsts, seconds)]
    stacked = jnp.zeros((8, 128), F32)
    for k in range(4):
        stacked = jnp.where(row8 == k, jnp.broadcast_to(masks[k], (8, 128)), stacked)
    rank = ranks(stacked)
    total = jnp.zeros((176, 384), F32)
    for k in range(4):
        raw, mask = raws[k], masks[k]
        other = firsts[k] + seconds[k] - expert
        logits = dot(router[...], raws[k][:, 0:128].astype(BF16))
        own = jnp.sum(jnp.where(row8 == expert, logits, 0.0), 0, keepdims=True)
        rest = jnp.sum(jnp.where(row8 == jnp.broadcast_to(other, (8, 128)), logits, 0.0), 0, keepdims=True)
        gap = jnp.broadcast_to(own - rest, (8, 128))
        hi = gap.astype(BF16).astype(F32)
        mid = (gap - hi).astype(BF16).astype(F32)
        low = gap - hi - mid
        ext = jnp.where(row8 == 0, hi, jnp.where(row8 == 1, mid, jnp.where(row8 == 2, low, 0.0)))
        sign = jnp.where(row8 == expert, 1.0, 0.0) - jnp.where(row8 == jnp.broadcast_to(other, (8, 128)), 1.0, 0.0)
        left = jnp.concatenate(
            [raw[0:72, 0:128], ext, raw[0:72, 128:256], jnp.zeros((8, 128), F32), sign, jnp.zeros((8, 128), F32)], 0
        ).astype(BF16)
        slot = jnp.where(mask > 0, rank[k : k + 1, :] + 96.0 * k, -1.0).astype(jnp.int32)
        place = jnp.where(iota((384, 128), 0) == jnp.broadcast_to(slot, (384, 128)), 1.0, 0.0).astype(BF16)
        total = total + dot(left, place, LAST)
    tok_out[...] = total[0:80].astype(BF16)
    cot_out[...] = total[80:160].astype(BF16)
    sgn_out[...] = total[160:168]


def distance(index, at, n):
    side = 1 - 2 * lax.rem(at, 2)
    return lax.rem(side * (index - at) + 2 * n, n)


def position(steps, at, n):
    side = 1 - 2 * lax.rem(at, 2)
    return lax.rem(at + side * steps + 2 * n, n)


def weights_body(at, wg_ref, wu_ref, wd_ref, g_out, u_out, d_out, wg, wu, wd, sems):
    copies = fetch((wg_ref, wu_ref, wd_ref), (wg, wu, wd), sems)
    eye = jnp.where(iota((192, 192), 0) == iota((192, 192), 1), 1.0, 0.0).astype(BF16)
    zero = jnp.zeros((8, 192), F32)
    zs = [distance(z, at[0], NZ) for z in range(NZ)]
    ys = [distance(y, at[1], NY) for y in range(NY)]
    for copy, w, out, z_first in zip(copies, (wg, wu, wd), (g_out, u_out, d_out), (False, False, True)):
        copy.wait()
        for h in range(2):
            tall = dot(w[:, 1152 * h : 1152 * h + 1152], eye, NT)
            for i in range(16):
                z, y = zs[4 * h + i // NY], ys[i % NY]
                index = z * NY + y if z_first else y * NZ + z
                out[index] = jnp.concatenate([tall[72 * i : 72 * i + 72], zero], 0).astype(BF16)


def forward_body(pieces, *refs):
    toks, wg, wu, wd = refs[:pieces], refs[pieces], refs[pieces + 1], refs[pieces + 2]
    gate_out, up_out, hid_out, gap_out = refs[pieces + 3 : pieces + 7]
    parts = refs[pieces + 7 :]
    gate = jnp.zeros((192, 384), F32)
    up = jnp.zeros((192, 384), F32)
    gap = jnp.zeros((8, 384), F32)
    at = 0
    for tok in toks:
        rows = tok.shape[0]
        x = tok[...]
        gate = gate + dot(wg[at : at + rows, :], x, NT)
        up = up + dot(wu[at : at + rows, :], x, NT)
        line = lax.rem(iota((8, rows), 1) + at, 80)
        pick = jnp.where((line >= 72) & (line < 75), 1.0, 0.0).astype(BF16)
        gap = gap + dot(pick, x)
        at += rows
    hidden = (gate * jax.nn.sigmoid(gate) * up).astype(BF16)
    gate_out[...] = gate
    up_out[...] = up
    hid_out[...] = hidden
    gap_out[...] = gap
    scale = jax.nn.sigmoid(gap[0:1, :])
    at = 0
    for part in parts:
        rows = part.shape[0]
        part[...] = (dot(wd[at : at + rows, :], hidden) * scale).astype(BF16)
        at += rows


def backward_body(pieces, *refs):
    cots = refs[:pieces]
    wg, wu, wd, gate_ref, up_ref, hid_ref, gap_ref = refs[pieces : pieces + 7]
    scaled_out, parts = refs[pieces + 7], refs[pieces + 8 :]
    dhid = jnp.zeros((192, 384), F32)
    at = 0
    for cot in cots:
        rows = cot.shape[0]
        dhid = dhid + dot(wd[at : at + rows, :], cot[...], NT)
        at += rows
    gap = gap_ref[0:1, :]
    first, second = jax.nn.sigmoid(gap), jax.nn.sigmoid(-gap)
    gate, up = gate_ref[...], up_ref[...]
    hidden = hid_ref[...].astype(F32)
    slope = jnp.sum(hidden * dhid, 0, keepdims=True) * first * second
    dhid = dhid * first
    sig = jax.nn.sigmoid(gate)
    grad_gate = (dhid * up * (sig * (1.0 + gate * (1.0 - sig)))).astype(BF16)
    grad_up = (dhid * (gate * sig)).astype(BF16)
    scaled_out[...] = (hidden * first).astype(BF16)
    at = 0
    for out in parts:
        rows = out.shape[0]
        part = dot(wg[at : at + rows, :], grad_gate) + dot(wu[at : at + rows, :], grad_up)
        line = lax.rem(iota((rows, 384), 0), 80)
        out[...] = jnp.where(line == 72, jnp.broadcast_to(slope, (rows, 384)), part).astype(BF16)
        at += rows


def down_body(pieces, at_ref, *refs):
    cots, scaled, out, held = refs[:pieces], refs[pieces], refs[pieces + 1], refs[pieces + 2]
    block = 0
    for cot in cots:
        part = dot(cot[...], scaled[...], LAST)
        for i in range(cot.shape[0] // 80):
            z = position(block // NY, at_ref[0], NZ)
            y = position(block % NY, at_ref[1], NY)
            held[z * NY + y] = part[80 * i : 80 * i + 72, :]
            block += 1
    eye = jnp.where(iota((192, 192), 0) == iota((192, 192), 1), 1.0, 0.0).astype(BF16)
    tall = held[...].reshape(2304, 192).astype(BF16)
    out[...] = dot(eye, tall, LAST).astype(BF16)


def copy_body(x, out):
    out[...] = x[...]


def grad_body(mine, other, out, done):
    out[...] = mine[...].astype(F32) + other[...].astype(F32)
    done[...] = jnp.zeros((8, 128), F32)


def finish_body(outs, grads, *refs):
    sgn, router, tok, p0, p1, p2, p3 = refs[outs + grads :]
    out, grad = total(refs[:outs]), total(refs[outs : outs + grads])
    delta = sgn[...] * grad[72:73, :]
    hi = delta.astype(BF16)
    low = (delta - hi.astype(F32)).astype(BF16)
    grad = grad + dot(router[...], hi, NT) + dot(router[...], low, NT)
    rows = jnp.concatenate([tok[...], jnp.zeros((48, 384), BF16)], 0)
    share = dot(hi, rows, LAST) + dot(low, rows, LAST)
    share_hi = share.astype(BF16).astype(F32)
    share_low = pltpu.roll(share - share_hi, 4, 0)
    extra = jnp.where(iota((8, 128), 0) < 4, share_hi, share_low)
    extra = jnp.concatenate([jnp.zeros((72, 128), F32), extra, jnp.zeros((80, 128), F32)], 0)
    both = jnp.concatenate([out, grad], 0).astype(BF16)
    slot, lane = iota((384, 128), 0), iota((384, 128), 1)
    for k, ref in enumerate((p0, p1, p2, p3)):
        pick = jnp.where((slot == lane + 96 * k) & (lane < 96), 1.0, 0.0).astype(BF16)
        ref[...] = (dot(both, pick) + extra).astype(BF16)


def share_body(r0, r1, r2, r3, out):
    share = total([r.at[64:80, :] for r in (r0, r1, r2, r3)])[8:16]
    out[...] = share + pltpu.roll(share, 4, 0)


def combine_body(me, ids, r0, r1, r2, r3, mixed_out, grad_out):
    row8 = iota((8, 128), 0)
    first = jnp.broadcast_to(ids[0:1, :], (8, 128))
    second = jnp.broadcast_to(ids[1:2, :], (8, 128))
    owner = lax.rem(me[0] - row8 + 8, 4)
    masks = jnp.where((first == owner) | (second == owner), 1.0, 0.0)
    rank = ranks(masks)
    slots = jnp.where(masks > 0, rank, -1.0).astype(jnp.int32)
    both = jnp.zeros((160, 128), F32)
    for k, ref in enumerate((r0, r1, r2, r3)):
        place = jnp.where(iota((128, 128), 0) == jnp.broadcast_to(slots[k : k + 1, :], (128, 128)), 1.0, 0.0)
        both = both + dot(ref[...], place.astype(BF16))
    mixed_out[...] = both[0:72].astype(BF16)
    grad_out[...] = both[80:152].astype(BF16)


def on_device(tokens, expert_ids, router, w_gate, w_up, w_down, cotangent):
    me = lax.axis_index("expert").astype(jnp.int32).reshape(1)
    t = lax.axis_index("tensor").astype(jnp.int32)
    at = jnp.stack([t // NY, t % NY])
    ids = expert_ids.T
    router_wide = jnp.pad(router.T, ((0, 4), (0, 8)))

    rows = jnp.concatenate([tokens.T, cotangent.T], 1)
    raw = jnp.concatenate([rows, jnp.pad(ids.astype(BF16), ((0, 6), (0, 128)))], 0)
    (even_z, odd_z, far_z), (even_y, odd_y, far_y) = swaps("z")[0], swaps("y")[0]
    wide = (32, 80, 192)

    raws = [raw] + [shift_x(raw, -k) for k in (1, 2, 3)]
    wg, wu, wd = call(
        weights_body, [(wide, BF16)] * 3, at, w_gate[0].T, w_up[0].T, w_down[0],
        scalars=1, far=3, limit=16, name="weights",
    )
    tok, cot, sgn = call(
        route_body,
        [((80, 384), BF16), ((80, 384), BF16), ((8, 384), F32)],
        me, *raws, router_wide, scalars=1, after=[wg], name="route",
    )
    wg, wu, wd = wg.reshape(2560, 192), wu.reshape(2560, 192), wd.reshape(2560, 192)

    tz1, tz7, tz4 = even_z(tok), odd_z(tok), far_z(tok)
    cy1, cy3, cy2 = even_y(cot), odd_y(cot), far_y(cot)
    cot_y = join([cot, cy1, cy2, cy3])
    tz2, tz6 = even_z(tz7), odd_z(tz1)
    a, b = relay(tz2, tz6, after=[cy1, cy2, cy3, tz4])
    tz3, tz5 = even_z(a), odd_z(b)
    tok_z = join([tok, tz1, tz2, tz3, tz4, tz5, tz6, tz7])
    ty1, ty3 = even_y(tok_z), odd_y(tok_z)
    cz1, cz7 = even_z(cot_y), odd_z(cot_y)
    cz2, cz6 = even_z(cz7), odd_z(cz1)
    a, b = cut(ty1, ty3, after=[cz2, cz6])
    ty2_low, ty2_high = even_y(a), odd_y(b)
    cz3, cz5 = even_z(cz6), odd_z(cz2)
    toks = [tok_z, ty1, ty2_low, ty2_high, ty3]

    square = (192, 384)
    gate, up, hidden, gap, *oz = call(
        lambda *r: forward_body(len(toks), *r),
        [(square, F32), (square, F32), (square, BF16), ((8, 384), F32)]
        + [((320 if i < 4 or i > 5 else 160, 384), BF16) for i in range(NZ + 1)],
        *toks, wg, wu, wd, flops=1200000000, limit=24, name="forward",
    )
    a, b = cut(cz3, cz5, after=[hidden])
    cz4_low, cz4_high = even_z(a), odd_z(b)
    cots = [cot_y, cz1, cz2, cz3, cz4_low, cz4_high, cz5, cz6, cz7]

    oz[4:6] = [oz[4:6]]
    c, d = even_z(oz[4][0]), odd_z(oz[4][1])
    scaled, *gy = call(
        lambda *r: backward_body(len(cots), *r),
        [(square, BF16)] + [((320 if i in (2, 3) else 640, 384), BF16) for i in range(NY + 1)],
        *cots, wg, wu, wd, gate, up, hidden, gap, flops=1200000000, limit=24, name="backward",
    )
    gy[2:4] = [gy[2:4]]
    a, b = add(oz[3], oz[5], c, d)
    e, f = even_y(gy[2][0]), odd_y(gy[2][1])
    g, h = add(gy[1], gy[3], e, f, after=[a])
    c, d = even_z(a), odd_z(b)
    (down,) = call(
        lambda *r: down_body(len(cots), *r),
        [((192, 2304), BF16)],
        at, *cots, scaled, scalars=1, flops=500000000, after=[g], extra=[((32, 72, 192), F32)],
        limit=16, name="down",
    )
    (mine,) = call(copy_body, [((192, 2304), BF16)], down, after=[c, d], name="copy")
    other = lax.ppermute(mine, "dp", [(0, 1), (1, 0)])
    a, b = add(oz[2], oz[6], c, d)
    e, f = even_y(g), odd_y(h)
    c, d = even_z(a), odd_z(b)
    gz = sum_blocks(gy[0], e, f)
    a, b = add(oz[1], oz[7], c, d)
    c, d = even_z(a), odd_z(b)
    e, f, gz_far = even_z(gz[3]), odd_z(gz[5]), far_z(gz[4])
    g, h = add(gz[2], gz[6], e, f)
    oy = sum_blocks(oz[0], c, d)
    outs = [oy[0], even_y(oy[1]), odd_y(oy[3]), far_y(oy[2])]
    e, f = even_z(g), odd_z(h)
    g, h = add(gz[1], gz[7], e, f)
    grads = [gz[0], gz_far, even_z(g), odd_z(h)]
    down_grad, done = call(
        grad_body, [((192, 2304), F32), ((8, 128), F32)], mine, other, home=True, limit=16, name="grad"
    )
    parts = call(
        lambda *r: finish_body(len(outs), len(grads), *r),
        [((160, 128), BF16)] * 4, *outs, *grads, sgn, router_wide, tok, name="finish",
    )
    back = [parts[0]] + [shift_x(parts[k], k) for k in (1, 2, 3)]
    (share,) = call(share_body, [((8, 128), F32)], *back, after=[done], name="share")
    mixed, token_grad = call(
        combine_body,
        [((72, 128), BF16), ((72, 128), BF16)],
        me, ids, *back, scalars=1, name="combine",
    )
    share = share + lax.ppermute(share, "dp", [(0, 1), (1, 0)])
    router_grad = share[:4, :72].T
    return mixed.T, token_grad.T, router_grad, down_grad[None]


def solution(mesh):
    in_specs = (
        P(("dp", "expert"), "tensor"),
        P(("dp", "expert"), None),
        P("tensor", None),
        P("expert", None, "tensor"),
        P("expert", None, "tensor"),
        P("expert", "tensor", None),
        P(("dp", "expert"), "tensor"),
    )
    out_specs = (
        P(("dp", "expert"), "tensor"),
        P(("dp", "expert"), "tensor"),
        P("tensor", None),
        P("expert", "tensor", None),
    )
    return jax.shard_map(
        on_device, mesh=mesh, in_specs=in_specs, out_specs=out_specs, check_vma=False
    )
```

```python
import jax
import jax.numpy as jnp
from jax import lax
from jax.experimental import pallas as pl
from jax.experimental.pallas import tpu as pltpu
from jax.sharding import PartitionSpec as P

F32 = jnp.float32
BF16 = jnp.bfloat16
NZ, NY = 8, 4
NT = (((0,), (0,)), ((), ()))
LAST = (((1,), (1,)), ((), ()))


def dot(a, b, dims=(((1,), (0,)), ((), ()))):
    return lax.dot_general(a, b, dims, preferred_element_type=F32)


def iota(shape, axis):
    return lax.broadcasted_iota(jnp.int32, shape, axis)


def call(body, outs, *args, scalars=0, flops=0, limit=8, far=0, after=(), home=False, extra=(), name=None):
    smem = pl.BlockSpec(memory_space=pltpu.SMEM)
    vmem = pl.BlockSpec(memory_space=pltpu.VMEM)
    count = len(args)
    near = count - scalars - far
    moved = sum(a.size * a.dtype.itemsize for a in args)
    scratch = [pltpu.VMEM(a.shape, a.dtype) for a in args[count - far :]]
    if far:
        scratch.append(pltpu.SemaphoreType.DMA((far,)))
    scratch += [pltpu.VMEM(shape, dtype) for shape, dtype in extra]
    return pl.pallas_call(
        lambda *refs: body(*refs[:count], *refs[count + len(after) :]),
        out_shape=tuple(jax.ShapeDtypeStruct(s, d) for s, d in outs),
        in_specs=[smem] * scalars + [vmem] * near + [pl.BlockSpec(memory_space=pltpu.HBM)] * far
        + [pl.BlockSpec(memory_space=pl.ANY)] * len(after),
        out_specs=tuple(pl.BlockSpec() if home else vmem for _ in outs),
        scratch_shapes=scratch,
        compiler_params=pltpu.CompilerParams(vmem_limit_bytes=limit * 1024 * 1024),
        cost_estimate=pl.CostEstimate(flops=flops, bytes_accessed=moved, transcendentals=0),
        name=name,
    )(*args, *after)


def fetch(refs, held, sems):
    copies = [pltpu.make_async_copy(r, h, sems.at[i]) for i, (r, h) in enumerate(zip(refs, held))]
    for copy in copies:
        copy.start()
    return copies


def shift_x(x, k):
    return lax.ppermute(x, "expert", [(i, (i + k) % 4) for i in range(4)])


def ring_pairs(n):
    even = [i ^ 1 for i in range(n)]
    odd = [(i + 1) % n if i % 2 else (i - 1) % n for i in range(n)]
    opposite = [(i + n // 2) % n for i in range(n)]
    return even, odd, opposite


def swaps(along):
    n = NZ if along == "z" else NY
    moves = []
    for partner in ring_pairs(n):
        if along == "z":
            pairs = [(z * NY + y, partner[z] * NY + y) for z in range(NZ) for y in range(NY)]
        else:
            pairs = [(z * NY + y, z * NY + partner[y]) for z in range(NZ) for y in range(NY)]
        moves.append(lambda x, pairs=pairs: lax.ppermute(x, "tensor", pairs))
    return moves, n


def halves(rows):
    return (rows // 2 + 15) // 16 * 16


def cut_body(a, b, low, high):
    cut = low.shape[0]
    low[...] = b[:cut, :]
    high[...] = a[cut:, :]


def cut(a, b, after=()):
    rows, width = a.shape
    first = halves(rows)
    shape = [((first, width), BF16), ((rows - first, width), BF16)]
    return call(cut_body, shape, a, b, after=after, name="cut")


def relay_body(a, b, a_out, b_out):
    a_out[...] = b[...]
    b_out[...] = a[...]


def relay(a, b, after):
    return call(relay_body, [(a.shape, BF16)] * 2, a, b, after=after, name="relay")


def join_body(parts, *refs):
    at = 0
    for ref in refs[:parts]:
        rows = ref.shape[0]
        refs[parts][at : at + rows, :] = ref[...]
        at += rows


def join(pieces, after=()):
    rows = sum(p.shape[0] for p in pieces)
    shape = [((rows, pieces[0].shape[1]), BF16)]
    return call(lambda *r: join_body(len(pieces), *r), shape, *pieces, after=after, name="join")[0]


def add_body(a, b, c, d, a_out, b_out):
    cut = c.shape[0]
    rest = a.shape[0] - d.shape[0]
    if rest:
        a_out[:rest, :] = a[:rest, :]
        b_out[cut:, :] = b[cut:, :]
    a_out[rest:, :] = (a[rest:, :].astype(F32) + d[...].astype(F32)).astype(BF16)
    b_out[:cut, :] = (b[:cut, :].astype(F32) + c[...].astype(F32)).astype(BF16)


def add(a, b, c, d, after=()):
    return call(add_body, [(a.shape, BF16)] * 2, a, b, c, d, after=after, name="add")


def total(terms):
    return sum(t[...].astype(F32) for t in terms)


def split_body(terms, *refs):
    for i, out in enumerate(refs[terms:]):
        out[...] = total([r.at[80 * i : 80 * i + 80, :] for r in refs[:terms]]).astype(BF16)


def sum_blocks(*terms, after=()):
    shape = [((80, 384), BF16)] * (terms[0].shape[0] // 80)
    return call(lambda *r: split_body(len(terms), *r), shape, *terms, after=after, name="sum")


def ranks(masks):
    earlier = (iota((128, 128), 0) < iota((128, 128), 1)).astype(F32).astype(BF16)
    return dot(masks.astype(BF16), earlier)


def route_body(me, r0, r1, r2, r3, router, tok_out, cot_out, sgn_out):
    expert = me[0].astype(F32)
    row8 = iota((8, 128), 0).astype(F32)
    raws = [r[...].astype(F32) for r in (r0, r1, r2, r3)]
    firsts = [r[72:73, 0:128] for r in raws]
    seconds = [r[73:74, 0:128] for r in raws]
    masks = [jnp.where((a == expert) | (b == expert), 1.0, 0.0) for a, b in zip(firsts, seconds)]
    stacked = jnp.zeros((8, 128), F32)
    for k in range(4):
        stacked = jnp.where(row8 == k, jnp.broadcast_to(masks[k], (8, 128)), stacked)
    rank = ranks(stacked)
    total = jnp.zeros((176, 384), F32)
    for k in range(4):
        raw, mask = raws[k], masks[k]
        other = firsts[k] + seconds[k] - expert
        logits = dot(router[...], raws[k][:, 0:128].astype(BF16))
        own = jnp.sum(jnp.where(row8 == expert, logits, 0.0), 0, keepdims=True)
        rest = jnp.sum(jnp.where(row8 == jnp.broadcast_to(other, (8, 128)), logits, 0.0), 0, keepdims=True)
        gap = jnp.broadcast_to(own - rest, (8, 128))
        hi = gap.astype(BF16).astype(F32)
        mid = (gap - hi).astype(BF16).astype(F32)
        low = gap - hi - mid
        ext = jnp.where(row8 == 0, hi, jnp.where(row8 == 1, mid, jnp.where(row8 == 2, low, 0.0)))
        sign = jnp.where(row8 == expert, 1.0, 0.0) - jnp.where(row8 == jnp.broadcast_to(other, (8, 128)), 1.0, 0.0)
        left = jnp.concatenate(
            [raw[0:72, 0:128], ext, raw[0:72, 128:256], jnp.zeros((8, 128), F32), sign, jnp.zeros((8, 128), F32)], 0
        ).astype(BF16)
        slot = jnp.where(mask > 0, rank[k : k + 1, :] + 96.0 * k, -1.0).astype(jnp.int32)
        place = jnp.where(iota((384, 128), 0) == jnp.broadcast_to(slot, (384, 128)), 1.0, 0.0).astype(BF16)
        total = total + dot(left, place, LAST)
    tok_out[...] = total[0:80].astype(BF16)
    cot_out[...] = total[80:160].astype(BF16)
    sgn_out[...] = total[160:168]


def distance(index, at, n):
    side = 1 - 2 * lax.rem(at, 2)
    return lax.rem(side * (index - at) + 2 * n, n)


def position(steps, at, n):
    side = 1 - 2 * lax.rem(at, 2)
    return lax.rem(at + side * steps + 2 * n, n)


def weights_body(z_first, at, w_ref, out, w, sems):
    (copy,) = fetch((w_ref,), (w,), sems)
    eye = jnp.where(iota((192, 192), 0) == iota((192, 192), 1), 1.0, 0.0).astype(BF16)
    zero = jnp.zeros((8, 192), F32)
    zs = [distance(z, at[0], NZ) for z in range(NZ)]
    ys = [distance(y, at[1], NY) for y in range(NY)]
    copy.wait()
    for h in range(2):
        tall = dot(w[:, 1152 * h : 1152 * h + 1152], eye, NT)
        for i in range(16):
            z, y = zs[4 * h + i // NY], ys[i % NY]
            index = z * NY + y if z_first else y * NZ + z
            out[index] = jnp.concatenate([tall[72 * i : 72 * i + 72], zero], 0).astype(BF16)


def forward_body(pieces, *refs):
    toks, wg, wu, wd = refs[:pieces], refs[pieces], refs[pieces + 1], refs[pieces + 2]
    gate_out, up_out, hid_out, gap_out = refs[pieces + 3 : pieces + 7]
    parts = refs[pieces + 7 :]
    gate = jnp.zeros((192, 384), F32)
    up = jnp.zeros((192, 384), F32)
    gap = jnp.zeros((8, 384), F32)
    at = 0
    for tok in toks:
        rows = tok.shape[0]
        x = tok[...]
        gate = gate + dot(wg[at : at + rows, :], x, NT)
        up = up + dot(wu[at : at + rows, :], x, NT)
        line = lax.rem(iota((8, rows), 1) + at, 80)
        pick = jnp.where((line >= 72) & (line < 75), 1.0, 0.0).astype(BF16)
        gap = gap + dot(pick, x)
        at += rows
    hidden = (gate * jax.nn.sigmoid(gate) * up).astype(BF16)
    gate_out[...] = gate
    up_out[...] = up
    hid_out[...] = hidden
    gap_out[...] = gap
    scale = jax.nn.sigmoid(gap[0:1, :])
    at = 0
    for part in parts:
        rows = part.shape[0]
        part[...] = (dot(wd[at : at + rows, :], hidden) * scale).astype(BF16)
        at += rows


def backward_body(pieces, *refs):
    cots = refs[:pieces]
    wg, wu, wd, gate_ref, up_ref, hid_ref, gap_ref = refs[pieces : pieces + 7]
    scaled_out, parts = refs[pieces + 7], refs[pieces + 8 :]
    dhid = jnp.zeros((192, 384), F32)
    at = 0
    for cot in cots:
        rows = cot.shape[0]
        dhid = dhid + dot(wd[at : at + rows, :], cot[...], NT)
        at += rows
    gap = gap_ref[0:1, :]
    first, second = jax.nn.sigmoid(gap), jax.nn.sigmoid(-gap)
    gate, up = gate_ref[...], up_ref[...]
    hidden = hid_ref[...].astype(F32)
    slope = jnp.sum(hidden * dhid, 0, keepdims=True) * first * second
    dhid = dhid * first
    sig = jax.nn.sigmoid(gate)
    grad_gate = (dhid * up * (sig * (1.0 + gate * (1.0 - sig)))).astype(BF16)
    grad_up = (dhid * (gate * sig)).astype(BF16)
    scaled_out[...] = (hidden * first).astype(BF16)
    at = 0
    for out in parts:
        rows = out.shape[0]
        part = dot(wg[at : at + rows, :], grad_gate) + dot(wu[at : at + rows, :], grad_up)
        line = lax.rem(iota((rows, 384), 0), 80)
        out[...] = jnp.where(line == 72, jnp.broadcast_to(slope, (rows, 384)), part).astype(BF16)
        at += rows


def down_body(pieces, at_ref, *refs):
    cots, scaled, out, held = refs[:pieces], refs[pieces], refs[pieces + 1], refs[pieces + 2]
    block = 0
    for cot in cots:
        part = dot(cot[...], scaled[...], LAST)
        for i in range(cot.shape[0] // 80):
            z = position(block // NY, at_ref[0], NZ)
            y = position(block % NY, at_ref[1], NY)
            held[z * NY + y] = part[80 * i : 80 * i + 72, :]
            block += 1
    eye = jnp.where(iota((192, 192), 0) == iota((192, 192), 1), 1.0, 0.0).astype(BF16)
    tall = held[...].reshape(2304, 192).astype(BF16)
    out[...] = dot(eye, tall, LAST).astype(BF16)


def copy_body(x, out):
    out[...] = x[...]


def grad_body(mine, other, out, done):
    out[...] = mine[...].astype(F32) + other[...].astype(F32)
    done[...] = jnp.zeros((8, 128), F32)


def finish_body(outs, grads, *refs):
    sgn, router, tok, p0, p1, p2, p3 = refs[outs + grads :]
    out, grad = total(refs[:outs]), total(refs[outs : outs + grads])
    delta = sgn[...] * grad[72:73, :]
    hi = delta.astype(BF16)
    low = (delta - hi.astype(F32)).astype(BF16)
    grad = grad + dot(router[...], hi, NT) + dot(router[...], low, NT)
    rows = jnp.concatenate([tok[...], jnp.zeros((48, 384), BF16)], 0)
    share = dot(hi, rows, LAST) + dot(low, rows, LAST)
    share_hi = share.astype(BF16).astype(F32)
    share_low = pltpu.roll(share - share_hi, 4, 0)
    extra = jnp.where(iota((8, 128), 0) < 4, share_hi, share_low)
    extra = jnp.concatenate([jnp.zeros((72, 128), F32), extra, jnp.zeros((80, 128), F32)], 0)
    both = jnp.concatenate([out, grad], 0).astype(BF16)
    slot, lane = iota((384, 128), 0), iota((384, 128), 1)
    for k, ref in enumerate((p0, p1, p2, p3)):
        pick = jnp.where((slot == lane + 96 * k) & (lane < 96), 1.0, 0.0).astype(BF16)
        ref[...] = (dot(both, pick) + extra).astype(BF16)


def share_body(r0, r1, r2, r3, out):
    share = total([r.at[64:80, :] for r in (r0, r1, r2, r3)])[8:16]
    out[...] = share + pltpu.roll(share, 4, 0)


def combine_body(me, ids, r0, r1, r2, r3, mixed_out, grad_out):
    row8 = iota((8, 128), 0)
    first = jnp.broadcast_to(ids[0:1, :], (8, 128))
    second = jnp.broadcast_to(ids[1:2, :], (8, 128))
    owner = lax.rem(me[0] - row8 + 8, 4)
    masks = jnp.where((first == owner) | (second == owner), 1.0, 0.0)
    rank = ranks(masks)
    slots = jnp.where(masks > 0, rank, -1.0).astype(jnp.int32)
    both = jnp.zeros((160, 128), F32)
    for k, ref in enumerate((r0, r1, r2, r3)):
        place = jnp.where(iota((128, 128), 0) == jnp.broadcast_to(slots[k : k + 1, :], (128, 128)), 1.0, 0.0)
        both = both + dot(ref[...], place.astype(BF16))
    mixed_out[...] = both[0:72].astype(BF16)
    grad_out[...] = both[80:152].astype(BF16)


def on_device(tokens, expert_ids, router, w_gate, w_up, w_down, cotangent):
    me = lax.axis_index("expert").astype(jnp.int32).reshape(1)
    t = lax.axis_index("tensor").astype(jnp.int32)
    at = jnp.stack([t // NY, t % NY])
    ids = expert_ids.T
    router_wide = jnp.pad(router.T, ((0, 4), (0, 8)))

    raw = jnp.pad(tokens.T, ((0, 8), (0, 128))) + jnp.pad(cotangent.T, ((0, 8), (128, 0)))
    raw = raw + jnp.pad(ids.astype(BF16), ((72, 6), (0, 128)))
    raws = [raw] + [shift_x(raw, -k) for k in (1, 2, 3)]
    (even_z, odd_z, far_z), (even_y, odd_y, far_y) = swaps("z")[0], swaps("y")[0]
    wide = (32, 80, 192)
    wg, wu, wd = [
        call(lambda *r, f=f: weights_body(f, *r), [(wide, BF16)], at, w, scalars=1, far=1, limit=8, name="weights")[0]
        for w, f in ((w_gate[0].T, False), (w_up[0].T, False), (w_down[0], True))
    ]
    tok, cot, sgn = call(
        route_body,
        [((80, 384), BF16), ((80, 384), BF16), ((8, 384), F32)],
        me, *raws, router_wide, scalars=1, after=[wg, wu, wd], name="route",
    )
    wg, wu, wd = wg.reshape(2560, 192), wu.reshape(2560, 192), wd.reshape(2560, 192)

    tz1, tz7, tz4 = even_z(tok), odd_z(tok), far_z(tok)
    cy1, cy3, cy2 = even_y(cot), odd_y(cot), far_y(cot)
    cot_y = join([cot, cy1, cy2, cy3])
    tz2, tz6 = even_z(tz7), odd_z(tz1)
    a, b = relay(tz2, tz6, after=[cy1, cy2, cy3, tz4])
    tz3, tz5 = even_z(a), odd_z(b)
    tok_z = join([tok, tz1, tz2, tz3, tz4, tz5, tz6, tz7])
    ty1, ty3 = even_y(tok_z), odd_y(tok_z)
    cz1, cz7 = even_z(cot_y), odd_z(cot_y)
    cz2, cz6 = even_z(cz7), odd_z(cz1)
    a, b = cut(ty1, ty3, after=[cz2, cz6])
    ty2_low, ty2_high = even_y(a), odd_y(b)
    cz3, cz5 = even_z(cz6), odd_z(cz2)
    toks = [tok_z, ty1, ty2_low, ty2_high, ty3]

    square = (192, 384)
    gate, up, hidden, gap, *oz = call(
        lambda *r: forward_body(len(toks), *r),
        [(square, F32), (square, F32), (square, BF16), ((8, 384), F32)]
        + [((320 if i < 4 or i > 5 else 160, 384), BF16) for i in range(NZ + 1)],
        *toks, wg, wu, wd, flops=1200000000, limit=24, name="forward",
    )
    a, b = cut(cz3, cz5, after=[hidden])
    cz4_low, cz4_high = even_z(a), odd_z(b)
    cots = [cot_y, cz1, cz2, cz3, cz4_low, cz4_high, cz5, cz6, cz7]

    oz[4:6] = [oz[4:6]]
    c, d = even_z(oz[4][0]), odd_z(oz[4][1])
    scaled, *gy = call(
        lambda *r: backward_body(len(cots), *r),
        [(square, BF16)] + [((320 if i in (2, 3) else 640, 384), BF16) for i in range(NY + 1)],
        *cots, wg, wu, wd, gate, up, hidden, gap, flops=1200000000, limit=24, name="backward",
    )
    gy[2:4] = [gy[2:4]]
    a, b = add(oz[3], oz[5], c, d)
    e, f = even_y(gy[2][0]), odd_y(gy[2][1])
    g, h = add(gy[1], gy[3], e, f, after=[a])
    c, d = even_z(a), odd_z(b)
    (down,) = call(
        lambda *r: down_body(len(cots), *r),
        [((192, 2304), BF16)],
        at, *cots, scaled, scalars=1, flops=500000000, after=[g], extra=[((32, 72, 192), F32)],
        limit=16, name="down",
    )
    (mine,) = call(copy_body, [((192, 2304), BF16)], down, after=[c, d], name="copy")
    other = lax.ppermute(mine, "dp", [(0, 1), (1, 0)])
    a, b = add(oz[2], oz[6], c, d)
    e, f = even_y(g), odd_y(h)
    c, d = even_z(a), odd_z(b)
    gz = sum_blocks(gy[0], e, f)
    a, b = add(oz[1], oz[7], c, d)
    c, d = even_z(a), odd_z(b)
    e, f, gz_far = even_z(gz[3]), odd_z(gz[5]), far_z(gz[4])
    g, h = add(gz[2], gz[6], e, f)
    oy = sum_blocks(oz[0], c, d)
    outs = [oy[0], even_y(oy[1]), odd_y(oy[3]), far_y(oy[2])]
    e, f = even_z(g), odd_z(h)
    g, h = add(gz[1], gz[7], e, f)
    grads = [gz[0], gz_far, even_z(g), odd_z(h)]
    down_grad, done = call(
        grad_body, [((192, 2304), F32), ((8, 128), F32)], mine, other, home=True, limit=16, name="grad"
    )
    parts = call(
        lambda *r: finish_body(len(outs), len(grads), *r),
        [((160, 128), BF16)] * 4, *outs, *grads, sgn, router_wide, tok, name="finish",
    )
    back = [parts[0]] + [shift_x(parts[k], k) for k in (1, 2, 3)]
    (share,) = call(share_body, [((8, 128), F32)], *back, after=[done], name="share")
    mixed, token_grad = call(
        combine_body,
        [((72, 128), BF16), ((72, 128), BF16)],
        me, ids, *back, scalars=1, name="combine",
    )
    share = share + lax.ppermute(share, "dp", [(0, 1), (1, 0)])
    router_grad = share[:4, :72].T
    return mixed.T, token_grad.T, router_grad, down_grad[None]


def solution(mesh):
    in_specs = (
        P(("dp", "expert"), "tensor"),
        P(("dp", "expert"), None),
        P("tensor", None),
        P("expert", None, "tensor"),
        P("expert", None, "tensor"),
        P("expert", "tensor", None),
        P(("dp", "expert"), "tensor"),
    )
    out_specs = (
        P(("dp", "expert"), "tensor"),
        P(("dp", "expert"), "tensor"),
        P("tensor", None),
        P("expert", "tensor", None),
    )
    return jax.shard_map(
        on_device, mesh=mesh, in_specs=in_specs, out_specs=out_specs, check_vma=False
    )
```
